128 devices in a mesh: group: 4 (over y_hi, core), wide: 32 (over z, y_lo, x).
Axes of the slice: x: 4, y: 4 (y_hi: 2, y_lo: 2; y = y_hi * 2 + y_lo), z: 4, core: 2. Of those that a mesh axis runs over, the one named last changes fastest.
Arguments:
- acts: bfloat16 [4, 8192, 1280], P('group', 'wide'), may hold values from -6 to 6
- block_in: bfloat16 [4, 1280, 2560], P('group'), may hold values from -0.15625 to 0.15625
- block_out: bfloat16 [4, 2560, 1280], P('group'), may hold values from -0.125 to 0.125
- adapt_in: bfloat16 [3, 1280, 640], replicated, may hold values from -0.15625 to 0.15625
- adapt_out: bfloat16 [3, 640, 1280], replicated, may hold values from -0.25 to 0.25
- owner: int32 [4, 8], replicated, may hold values from 0 to 7, each once within a row
Outputs:
- grad_adapt_in: float32 [4, 1280, 640], P('group', 'wide')
- grad_adapt_out: float32 [4, 640, 1280], P('group', 'wide')
- grad_block_in: float32 [4, 1280, 2560], P('group', 'wide')
- grad_block_out: float32 [4, 2560, 1280], P('group', 'wide')
The draws below stay inside these ranges and needn't reach their ends.
Inputs may be any that keep to these rules, and one draw needn't show every extreme that they name: `owner`: each row is a permutation of the image numbers.
All inputs are finite; a program needn't handle non-finite values.
Results may differ from the reference program's by a relative error of at most 0.011.
Values may be sent and summed in bfloat16 or wider, within the bound.
No kernel may reach another device: no remote copies, remote signals or barrier semaphores. Data moves between devices by JAX's collectives and lax.ppermute only.
A program may use at most 128 MiB of HBM per device.

```python
import jax
import jax.numpy as jnp
from jax import lax

D = 1280
FF = 2560
AH = 640
PATCHES = 1024
TOK_DEV = 256
IMAGES = 8
TOKENS = 8192
N_WIDE = 32


def block_scale(stream_key, shape, cuts, least, top_value):
    def one(position, blocks):
        draws = jax.random.uniform(jax.random.fold_in(jax.random.fold_in(stream_key, 6), position), (blocks,), jnp.float32, least / len(cuts), top_value / len(cuts))
        return jnp.repeat(jnp.exp(draws), shape[position] // blocks).reshape((-1,) + (1,) * (len(shape) - position - 1))

    level = one(*cuts[0])
    for cut in cuts[1:]:
        level = level * one(*cut)
    return level


def gaussian(rng, dims, scale, bound, cuts=(), held_as=jnp.bfloat16):
    values = scale * jax.random.normal(rng, dims, jnp.float32)
    if cuts:
        values = values * block_scale(rng, dims, cuts, -0.22, 0.18)
    return jnp.clip(values, -bound, bound).astype(held_as)


def setup_inputs(seed: int = 0) -> dict:
    seeds = jax.random.split(jax.random.key(seed), 7)
    return {
        "acts": gaussian(seeds[0], (4, TOKENS, D), 1.0, 6.0, ((0, 4), (1, 32))),
        "block_in": gaussian(seeds[1], (4, D, FF), D ** -0.5, 0.15625, ((0, 4),)),
        "block_out": gaussian(seeds[2], (4, FF, D), FF ** -0.5, 0.125, ((0, 4),)),
        "adapt_in": gaussian(seeds[3], (3, D, AH), D ** -0.5, 0.15625),
        "adapt_out": gaussian(seeds[4], (3, AH, D), AH ** -0.5, 0.25),
        "owner": jax.vmap(lambda own: jax.random.permutation(own, IMAGES))(jax.random.split(seeds[5], 4)).reshape((4, IMAGES)).astype(jnp.int32),
    }


EPS = 1e-06

def block_forward(inputs, w_first, w_second):
    values = inputs.astype(jnp.float32)
    center = values - lax.optimization_barrier(jnp.mean(values, axis=-1, keepdims=True))
    spread = lax.optimization_barrier(jnp.mean(center * center, axis=-1, keepdims=True))
    normed = (center * lax.rsqrt(spread + EPS)).astype(jnp.bfloat16)
    before = jnp.dot(normed, w_first, preferred_element_type=jnp.float32)
    hidden = jax.nn.gelu(before, approximate=True).astype(jnp.bfloat16)
    output = (values + jnp.dot(hidden, w_second, preferred_element_type=jnp.float32)).astype(jnp.bfloat16)
    return (normed, before, hidden, output)

def token_loss(predicted, target):
    width = predicted.shape[-1]
    inner = lax.optimization_barrier(jnp.mean(predicted * target, axis=-1))
    first = lax.optimization_barrier(jnp.mean(predicted * predicted, axis=-1)) + EPS
    second = lax.optimization_barrier(jnp.mean(target * target, axis=-1)) + EPS
    cosine = inner * lax.rsqrt(first * second)
    differ = predicted - target
    return jnp.sum(width * (1.0 - cosine) + lax.optimization_barrier(jnp.sum(differ * differ, axis=-1)))

def contract_rows(left, right):
    return lax.dot_general(left, right, (((0,), (0,)), ((), ())), preferred_element_type=jnp.float32)

def contract_cols(left, right):
    return lax.dot_general(left, right, (((1,), (1,)), ((), ())), preferred_element_type=jnp.float32)

def gelu_grad(point, upstream):
    pull = jax.vjp(lambda z: jax.nn.gelu(z, approximate=True), point)[1]
    return pull(upstream)[0]

def adaptor_pass(student, target, a_first, a_second, loss_scale):
    zeta = jnp.dot(student, a_first, preferred_element_type=jnp.float32)
    gamma = jax.nn.gelu(zeta, approximate=True).astype(jnp.bfloat16)
    predicted = jnp.dot(gamma, a_second, preferred_element_type=jnp.float32)
    pull = jax.vjp(lambda p: token_loss(p, target), predicted)[1]
    grad_pred = pull(jnp.asarray(loss_scale, jnp.float32))[0]
    return (zeta, gamma, grad_pred)

def adaptor_back(zeta, grad_pred_b, a_first, a_second):
    grad_gamma = contract_cols(grad_pred_b, a_second)
    grad_zeta = gelu_grad(zeta, grad_gamma).astype(jnp.bfloat16)
    grad_student = contract_cols(grad_zeta, a_first)
    return (grad_zeta, grad_student)

def device_sum(left, right):
    left_blocks = left.reshape(N_WIDE, TOK_DEV, left.shape[1])
    right_blocks = right.reshape(N_WIDE, TOK_DEV, right.shape[1])

    def step(carry, pair):
        return (carry + contract_rows(pair[0], pair[1]), None)
    start = jnp.zeros((left.shape[1], right.shape[1]), jnp.float32)
    total, _ = lax.scan(step, start, (left_blocks, right_blocks))
    return total

def reference(acts, block_in, block_out, adapt_in, adapt_out, owner):
    per_image = PATCHES // TOK_DEV
    piece = TOK_DEV // N_WIDE
    row_ids = jnp.arange(TOKENS, dtype=jnp.int32)
    device_ids = row_ids // TOK_DEV
    inner_ids = row_ids % TOK_DEV
    block_ids = inner_ids // piece
    student_global = (owner[3][block_ids // per_image] * PATCHES + block_ids % per_image * TOK_DEV + device_ids * piece + inner_ids % piece).astype(jnp.int32)
    loss_scale = 1.0 / TOKENS ** 0.5
    outs = [block_forward(acts[g], block_in[g], block_out[g]) for g in range(4)]
    student_whole = jnp.zeros((TOKENS, D), jnp.bfloat16).at[student_global].set(outs[3][3])
    grad_whole = jnp.zeros((TOKENS, D), jnp.float32)
    grads_first = []
    grads_second = []
    for g in range(3):
        teacher_global = (owner[g][device_ids // per_image] * PATCHES + device_ids % per_image * TOK_DEV + inner_ids).astype(jnp.int32)
        student = student_whole[teacher_global]
        target = outs[g][3].astype(jnp.float32)
        zeta, gamma, grad_pred = adaptor_pass(student, target, adapt_in[g], adapt_out[g], loss_scale)
        grad_pred_b = grad_pred.astype(jnp.bfloat16)
        grad_zeta, grad_student = adaptor_back(zeta, grad_pred_b, adapt_in[g], adapt_out[g])
        grads_second.append(device_sum(gamma, grad_pred_b))
        grads_first.append(device_sum(student, grad_zeta))
        grad_whole = grad_whole.at[teacher_global].add(grad_student)
    grad_out = grad_whole[student_global].astype(jnp.bfloat16)
    normed, before, hidden, output = outs[3]
    grad_hidden = contract_cols(grad_out, block_out[3])
    grad_before = gelu_grad(before, grad_hidden).astype(jnp.bfloat16)
    student_second = device_sum(hidden, grad_out)
    student_first = device_sum(normed, grad_before)
    grad_adapt_in = jnp.stack(grads_first + [jnp.zeros((D, AH), jnp.float32)])
    grad_adapt_out = jnp.stack(grads_second + [jnp.zeros((AH, D), jnp.float32)])
    zero_first = jnp.zeros((D, FF), jnp.float32)
    zero_second = jnp.zeros((FF, D), jnp.float32)
    grad_block_in = jnp.stack([zero_first, zero_first, zero_first, student_first])
    grad_block_out = jnp.stack([zero_second, zero_second, zero_second, student_second])
    return (grad_adapt_in, grad_adapt_out, grad_block_in, grad_block_out)
```

```python
import functools

import jax
import jax.numpy as jnp
from jax import lax
from jax.experimental import pallas as pl
from jax.experimental.pallas import tpu as pltpu
from jax.sharding import Mesh
from jax.sharding import PartitionSpec as P

PATCHES = 1024


EPS = 1e-06
WIDE = ("z", "yl", "x")
GROUP = ("yh", "core")
ALL = GROUP + WIDE
SIZES = (2, 2, 4, 2, 4)
MIB = 1024 * 1024
BF16 = jnp.bfloat16


def cost(flops, moved):
    return pl.CostEstimate(flops=flops, bytes_accessed=moved, transcendentals=0)


F32 = jnp.float32
CORE, FLIP, GROUP_AT, CHOSEN, YL, KEEP, FIRST, SECOND = range(8)


def route(move):
    pairs = []
    for flat in range(128):
        x, yl, z, core, yh = flat % 4, flat // 4 % 2, flat // 8 % 4, flat // 32 % 2, flat // 64
        to = move(yh, core, z, yl, x)
        if to is not None:
            yh, core, z, yl, x = to
            pairs.append((flat, (((yh * 2 + core) * 4 + z % 4) * 2 + yl) * 4 + x % 4))
    return pairs


def send(value, move):
    return lax.ppermute(value, ALL, route(move))


def vmem(count):
    return [pl.BlockSpec(memory_space=pltpu.VMEM)] * count


def smem():
    return pl.BlockSpec(memory_space=pltpu.SMEM)


def in_hbm(*weights):
    return [pltpu.with_memory_space_constraint(w, pltpu.HBM) for w in weights]


def shaped(shape, dtype):
    return jax.ShapeDtypeStruct(shape, dtype)


def call(kernel, scalars, inputs, outputs, scratch=(), grant=16, flops=0):
    moved = sum(a.size * a.dtype.itemsize for a in (*inputs, *outputs))
    return pl.pallas_call(
        kernel,
        out_shape=list(outputs),
        in_specs=[smem()] + vmem(len(inputs)),
        out_specs=vmem(len(outputs)),
        scratch_shapes=list(scratch),
        compiler_params=pltpu.CompilerParams(vmem_limit_bytes=grant * MIB),
        cost_estimate=cost(flops, moved),
    )(scalars, *inputs)


def contract_rows(left, right):
    return lax.dot_general(
        left, right, (((0,), (0,)), ((), ())), preferred_element_type=F32
    )


def contract_cols(left, right):
    return lax.dot_general(
        left, right, (((1,), (1,)), ((), ())), preferred_element_type=F32
    )


def gelu_parts(point):
    root = 0.7978845608028654
    square = point * point
    bent = jnp.tanh(root * (point + 0.044715 * point * square))
    share = 0.5 * (1.0 + bent)
    slope = share + 0.5 * point * (1.0 - bent * bent) * (root * (1.0 + 0.134145 * square))
    return point * share, slope


CHUNK = 512


def forward_kernel(
    at, acts_hbm, first_hbm, second_hbm, hidden_hbm, hand_hbm, slope_hbm, out_ref, sent_ref,
    acts_ref, first_ref, second_ref, total, hidden_ref, normed_ref, slope_ref,
    first_sem, second_sem, hidden_sem, slope_sem, other_sem,
):
    tokens, hidden_width = slope_ref.shape
    width = out_ref.shape[1]
    count = hidden_width // CHUNK

    def first_copy(j):
        cut = pl.ds(j * CHUNK, CHUNK)
        return pltpu.make_async_copy(
            first_hbm.at[0, :, cut], first_ref.at[j], first_sem.at[j]
        )

    def second_copy(j):
        cut = pl.ds(j * CHUNK, CHUNK)
        return pltpu.make_async_copy(
            second_hbm.at[0, cut, :], second_ref.at[j], second_sem.at[j]
        )

    def hidden_copy(j):
        cut = pl.ds(j * CHUNK, CHUNK)
        return pltpu.make_async_copy(
            hidden_ref.at[:, cut], hidden_hbm.at[:, cut], hidden_sem.at[j]
        )

    def slope_copy(part):
        cut = pl.ds(part * (hidden_width // 2), hidden_width // 2)
        target = slope_hbm if part else hand_hbm.at[pl.ds(width + tokens, tokens)]
        return pltpu.make_async_copy(slope_ref.at[:, cut], target, slope_sem.at[part])

    def weight_copy(j):
        rows = min(CHUNK, width - j * CHUNK)
        return pltpu.make_async_copy(
            second_ref.at[j, pl.ds(0, rows)],
            hand_hbm.at[pl.ds(j * CHUNK, rows)],
            other_sem.at[2 + j],
        )

    acts_copy = pltpu.make_async_copy(acts_hbm.at[0], acts_ref, other_sem.at[0])
    normed_copy = pltpu.make_async_copy(
        normed_ref, hand_hbm.at[pl.ds(width, tokens)], other_sem.at[1]
    )
    acts_copy.start()
    first_copy(0).start()
    second_copy(0).start()
    first_copy(1).start()
    acts_copy.wait()
    values = acts_ref[...].astype(F32)
    center = values - jnp.mean(values, axis=-1, keepdims=True)
    spread = jnp.mean(center * center, axis=-1, keepdims=True)
    normed = (center * lax.rsqrt(spread + EPS)).astype(BF16)
    normed_ref[...] = normed
    normed_copy.start()
    total[...] = values
    first_copy(0).wait()
    before = jnp.dot(normed, first_ref[0], preferred_element_type=F32)
    for j in range(count):
        if j + 1 < count:
            second_copy(j + 1).start()
        if j + 2 < count:
            first_copy(j + 2).start()
        second_copy(j).wait()
        if j * CHUNK < width:
            weight_copy(j).start()
        if j + 1 < count:
            first_copy(j + 1).wait()
            later = jnp.dot(normed, first_ref[j + 1], preferred_element_type=F32)
        else:
            later = None
        hidden, slope = gelu_parts(before)
        hidden = hidden.astype(BF16)
        slope_ref[:, j * CHUNK : (j + 1) * CHUNK] = slope.astype(BF16)
        hidden_ref[:, j * CHUNK : (j + 1) * CHUNK] = hidden
        hidden_copy(j).start()
        if j == count // 2:
            slope_copy(0).start()
        total[...] += jnp.dot(hidden, second_ref[j], preferred_element_type=F32)
        before = later
    slope_copy(1).start()
    out_ref[...] = total[...].astype(BF16)
    for block in range(8):
        source = jnp.where(at[FLIP] == 1, block ^ 1, block) * 32
        sent_ref[block * 32 : block * 32 + 32] = total[
            pl.ds(pl.multiple_of(source, 32), 32)
        ].astype(BF16)
    for j in range(count):
        hidden_copy(j).wait()
        if j * CHUNK < width:
            weight_copy(j).wait()
    for part in range(2):
        slope_copy(part).wait()
    normed_copy.wait()


def block_forward(scalars, acts, block_in, block_out):
    _, tokens, width = acts.shape
    hidden = block_in.shape[2]
    count = hidden // CHUNK
    return pl.pallas_call(
        forward_kernel,
        out_shape=[
            pltpu.HBM((tokens, hidden), BF16),
            pltpu.HBM((hidden // 2 + 2 * tokens, width), BF16),
            pltpu.HBM((tokens, hidden // 2), BF16),
            shaped((tokens, width), BF16),
            shaped((tokens, width), BF16),
        ],
        in_specs=[smem()] + [pl.BlockSpec(memory_space=pltpu.HBM)] * 3,
        out_specs=[pl.BlockSpec(memory_space=pltpu.HBM)] * 3 + vmem(2),
        scratch_shapes=[
            pltpu.VMEM((tokens, width), BF16),
            pltpu.VMEM((count, width, CHUNK), BF16),
            pltpu.VMEM((count, CHUNK, width), BF16),
            pltpu.VMEM((tokens, width), F32),
            pltpu.VMEM((tokens, hidden), BF16),
            pltpu.VMEM((tokens, width), BF16),
            pltpu.VMEM((tokens, hidden), BF16),
            pltpu.SemaphoreType.DMA((count,)),
            pltpu.SemaphoreType.DMA((count,)),
            pltpu.SemaphoreType.DMA((count,)),
            pltpu.SemaphoreType.DMA((count,)),
            pltpu.SemaphoreType.DMA((2 + count,)),
        ],
        compiler_params=pltpu.CompilerParams(vmem_limit_bytes=32 * MIB),
        cost_estimate=cost(4 * tokens * width * hidden, 16777216),
    )(scalars, *in_hbm(acts, block_in, block_out))


def weight_copies(at, first_hbm, second_hbm, first_ref, second_ref, sems):
    first = pltpu.make_async_copy(first_hbm.at[at[CHOSEN]], first_ref, sems.at[0])
    second = pltpu.make_async_copy(second_hbm.at[at[CHOSEN]], second_ref, sems.at[1])
    return first, second


def pick_kernel(at, own_ref, crossed_ref, shared_ref):
    @pl.when(at[FLIP] == 0)
    def _():
        shared_ref[...] = own_ref[...]

    @pl.when(at[FLIP] == 1)
    def _():
        shared_ref[...] = crossed_ref[...]


def adapt_forward_kernel(
    at, shared_ref, handed_ref, first_hbm, second_hbm,
    student_ref, gamma_ref, mixed_ref, first_ref, second_ref, sems,
):
    first, second = weight_copies(at, first_hbm, second_hbm, first_ref, second_ref, sems)
    first.start()
    second.start()
    for core, source in enumerate((handed_ref, shared_ref)):

        @pl.when(at[CORE] == core)
        def _(source=source):
            student_ref[...] = source[...]

    first.wait()
    zeta = jnp.dot(student_ref[...], first_ref[...], preferred_element_type=F32)
    gamma, slope = gelu_parts(zeta)
    gamma = gamma.astype(BF16)
    gamma_ref[...] = gamma
    mixed_ref[:, 1280:] = slope
    second.wait()
    mixed_ref[:, :1280] = jnp.dot(gamma, second_ref[...], preferred_element_type=F32)


def adapt_call(kernel, scalars, inputs, adapt_in, adapt_out, outputs):
    return pl.pallas_call(
        kernel,
        out_shape=list(outputs),
        in_specs=[smem()] + vmem(len(inputs)) + [pl.BlockSpec(memory_space=pl.ANY)] * 2,
        out_specs=vmem(len(outputs)),
        scratch_shapes=[
            pltpu.VMEM(adapt_in.shape[1:], BF16),
            pltpu.VMEM(adapt_out.shape[1:], BF16),
            pltpu.SemaphoreType.DMA((2,)),
        ],
        compiler_params=pltpu.CompilerParams(vmem_limit_bytes=24 * MIB),
        cost_estimate=cost(1024, 1024),
    )(scalars, *inputs, *in_hbm(adapt_in, adapt_out))


def adapt_backward_kernel(
    scale, at, sorter_ref, arrived_ref, mixed_ref, first_hbm, second_hbm,
    grad_pred_ref, grad_zeta_ref, kept_ref, given_ref, first_ref, second_ref, sems,
):
    first_copy, second_copy = weight_copies(
        at, first_hbm, second_hbm, first_ref, second_ref, sems
    )
    second_copy.start()
    first_copy.start()
    target = jnp.dot(sorter_ref[...], arrived_ref[...], preferred_element_type=F32)
    pred = mixed_ref[:, :1280]
    inner = jnp.mean(pred * target, axis=-1, keepdims=True)
    first = jnp.mean(pred * pred, axis=-1, keepdims=True) + EPS
    second = jnp.mean(target * target, axis=-1, keepdims=True) + EPS
    turn = lax.rsqrt(first * second)
    grad_pred = scale * (2.0 * (pred - target) - turn * (target - (inner / first) * pred))
    grad_pred = grad_pred.astype(BF16)
    grad_pred_ref[...] = grad_pred
    second_copy.wait()
    grad_gamma = contract_cols(grad_pred, second_ref[...])
    grad_zeta = (grad_gamma * mixed_ref[:, 1280:]).astype(BF16)
    grad_zeta_ref[...] = grad_zeta
    first_copy.wait()
    grad = contract_cols(grad_zeta, first_ref[...])
    grad = jnp.where(at[GROUP_AT] < 3, grad, 0.0)

    @pl.when(at[CORE] == 0)
    def _():
        kept_ref[...] = grad[:128]
        given_ref[...] = grad[128:].astype(BF16)

    @pl.when(at[CORE] == 1)
    def _():
        kept_ref[...] = grad[128:]
        given_ref[...] = grad[:128].astype(BF16)


def pair_kernel(at, kept_ref, came_ref, pair_ref, sent_ref):
    pair = kept_ref[...] + came_ref[...].astype(F32)
    pair_ref[...] = pair
    sent_ref[...] = pair.astype(BF16)


def half_kernel(at, pair_ref, across_ref, out_ref):
    out_ref[...] = (pair_ref[...] + across_ref[...].astype(F32)).astype(BF16)


def join_halves(at, mine_ref, other_ref, joined):
    @pl.when(at[CORE] == 0)
    def _():
        joined[:128] = mine_ref[...]
        joined[128:] = other_ref[...]

    @pl.when(at[CORE] == 1)
    def _():
        joined[:128] = other_ref[...]
        joined[128:] = mine_ref[...]


def hand_out(at, terms, turn, keep_ref, give_ref, columns=slice(None)):
    for place in range(8):
        for ref, lines in ((keep_ref, (0, turn ^ 2)), (give_ref, (turn, 2))):
            for slot, mask in enumerate(lines):
                line = at[FIRST] ^ mask
                wide = jnp.where(
                    at[CORE] == 0, place * 4 + line, line * 8 + place % 2 * 4 + place // 2
                )
                ref[slot, place] = terms[wide, :, columns].astype(BF16)


def stage_kernel(
    at, crossed_hbm, crossed_core_hbm, hand_hbm, hand_core_hbm, slope_hbm, second_hbm,
    left, slope, weight, sems,
):
    tokens, width = slope.shape
    weight_part = pl.ds(0, width)
    normed_part, slope_part = pl.ds(width, tokens), pl.ds(width + tokens, tokens)

    def student_copies(normed, slopes, weights):
        copies = (
            pltpu.make_async_copy(normed, left.at[:, pl.ds(0, width)], sems.at[0]),
            pltpu.make_async_copy(slopes, slope, sems.at[1]),
            pltpu.make_async_copy(weights, weight, sems.at[2]),
        )
        for copy in copies:
            copy.start()
        for copy in copies:
            copy.wait()

    for core, source in enumerate((crossed_core_hbm, crossed_hbm)):

        @pl.when((at[FLIP] == 1) & (at[CORE] == core))
        def _(source=source):
            copy = pltpu.make_async_copy(source, left, sems.at[0])
            copy.start()
            copy.wait()

    @pl.when((at[FLIP] == 0) & (at[CORE] == 0))
    def _():
        student_copies(
            hand_core_hbm.at[normed_part],
            hand_core_hbm.at[slope_part],
            hand_core_hbm.at[weight_part],
        )

    @pl.when((at[FLIP] == 0) & (at[CORE] == 1))
    def _():
        student_copies(
            hand_hbm.at[normed_part], slope_hbm, second_hbm.at[0, pl.ds(width, width), :]
        )


def stage(scalars, sources):
    tokens, width = sources[4].shape
    return pl.pallas_call(
        stage_kernel,
        out_shape=[
            shaped((tokens, 2 * width), BF16),
            shaped((tokens, width), BF16),
            shaped((width, width), BF16),
        ],
        in_specs=[smem()] + [pl.BlockSpec(memory_space=pltpu.HBM)] * 6,
        out_specs=vmem(3),
        scratch_shapes=[pltpu.SemaphoreType.DMA((3,))],
        compiler_params=pltpu.CompilerParams(vmem_limit_bytes=16 * MIB),
        cost_estimate=cost(0, 8388608),
    )(scalars, *in_hbm(*sources))


def student_kernel(
    at, left, slope, weight, mine_ref, other_ref, keep_a, give_a, keep_b, give_b, joined, before, terms
):
    join_halves(at, mine_ref, other_ref, joined)

    @pl.when(at[FLIP] == 1)
    def _():
        right = jnp.where(at[CORE] == 0, joined[:, :640], joined[:, 640:])
        for start in range(0, 2560, 640):
            block = contract_rows(left[:, start : start + 640], right)
            for index in range(8):
                row = index * 80
                terms[start // 80 + index, :, :640] = block[row : row + 40].astype(BF16)
                terms[start // 80 + index, :, 640:] = block[row + 40 : row + 80].astype(BF16)

    @pl.when(at[FLIP] == 0)
    def _():
        for start in range(0, 1280, 640):
            cut = slice(start, start + 640)
            grad_hidden = contract_cols(joined[...], weight[cut])
            before[:, cut] = (grad_hidden * slope[:, cut].astype(F32)).astype(BF16)
        for start in range(0, 1280, 640):
            block = contract_rows(left[:, start : start + 640], before[...]).astype(BF16)
            for index in range(16):
                terms[start // 40 + index] = block[index * 40 : index * 40 + 40]

    hand_out(at, terms, 1, keep_a, give_a, slice(0, 640))
    hand_out(at, terms, 3, keep_b, give_b, slice(640, 1280))


def student_partial(scalars, staged, mine, other):
    half, width = mine.shape
    tokens = 2 * half
    return call(
        student_kernel,
        scalars,
        (*staged, mine, other),
        [shaped((2, 8, 40, 640), BF16)] * 4,
        [
            pltpu.VMEM((tokens, width), BF16),
            pltpu.VMEM((tokens, width), BF16),
            pltpu.VMEM((32, 40, 1280), BF16),
        ],
        24,
        4 * tokens * width * width,
    )


def adapt_partial_kernel(
    at, student_ref, grad_zeta_ref, gamma_ref, grad_pred_ref, keep_a, give_a, keep_b, give_b, terms
):
    first = contract_rows(student_ref[...], grad_zeta_ref[...])
    second = contract_rows(gamma_ref[...], grad_pred_ref[...])
    for wide in range(32):
        terms[wide, :, :640] = first[wide * 40 : wide * 40 + 40]
        terms[wide, :20, 640:] = second[wide * 20 : wide * 20 + 20, :640]
        terms[wide, 20:, 640:] = second[wide * 20 : wide * 20 + 20, 640:]
    hand_out(at, terms, 1, keep_a, give_a, slice(0, 640))
    hand_out(at, terms, 3, keep_b, give_b, slice(640, 1280))


def next_kernel(at, keep_ref, came_ref, give_ref):
    give_ref[...] = (keep_ref[1].astype(F32) + came_ref[1].astype(F32)).astype(BF16)


def next_two_kernel(at, keep_a, came_a, keep_b, came_b, give_a, give_b):
    give_a[...] = (keep_a[1].astype(F32) + came_a[1].astype(F32)).astype(BF16)
    give_b[...] = (keep_b[1].astype(F32) + came_b[1].astype(F32)).astype(BF16)


def axis_two_kernel(
    turn, at, keep_a, came_a, last_a, keep_b, came_b, last_b, next_keep_ref, next_give_ref, total
):
    total[:, :, :640] = (
        keep_a[0].astype(F32) + came_a[0].astype(F32) + last_a[...].astype(F32)
    )
    total[:, :, 640:] = (
        keep_b[0].astype(F32) + came_b[0].astype(F32) + last_b[...].astype(F32)
    )
    for ref, lines in ((next_keep_ref, (0, turn ^ 2)), (next_give_ref, (turn, 2))):
        for slot, mask in enumerate(lines):
            line = at[SECOND] ^ mask
            for yl in range(2):
                ref[slot, yl] = total[line * 2 + yl].astype(ref.dtype)


def total_kernel(own_at, at, keep, came, last, mine_ref, given_ref, total):
    total[...] = keep[0] + came[0].astype(F32) + last[...].astype(F32)
    mine_ref[...] = total[at[own_at]]
    given_ref[...] = total[1 - at[own_at]].astype(BF16)


def piece_kernel(at, mine_ref, beside_ref, piece_ref, sent_ref):
    piece = mine_ref[...] + beside_ref[...].astype(F32)
    piece_ref[...] = piece
    sent_ref[...] = piece.astype(BF16)


def adapt_last_kernel(at, mine_ref, beside_ref, first_ref, second_ref):
    total = mine_ref[...] + beside_ref[...].astype(F32)
    total = jnp.where(at[GROUP_AT] < 3, total, 0.0)
    first_ref[0] = total[:, :640]
    second_ref[0, :, :640] = total[:20, 640:]
    second_ref[0, :, 640:] = total[20:, 640:]


def last_kernel(at, high_ref, low_ref, out_low_ref, out_high_ref, in_ref, out_ref):
    student = at[GROUP_AT] == 3
    in_ref[0, :, :1280] = jnp.where(student, low_ref[...], 0.0)
    in_ref[0, :, 1280:] = jnp.where(student, high_ref[...], 0.0)
    for start, ref in ((0, out_low_ref), (640, out_high_ref)):
        total = jnp.where(student, ref[...].astype(F32), 0.0)
        out_ref[0, :40, start : start + 640] = total[:, :640]
        out_ref[0, 40:, start : start + 640] = total[:, 640:]


def first_axis(mask):
    def to(yh, core, z, yl, x):
        return (yh, core, z, yl, x ^ mask) if core == 0 else (yh, core, z ^ mask, yl, x)

    return to


def second_axis(mask):
    def to(yh, core, z, yl, x):
        return (yh, core, z ^ mask, yl, x) if core == 0 else (yh, core, z, yl, x ^ mask)

    return to


def beside(yh, core, z, yl, x):
    return (yh, core, z, 1 - yl, x)


def first_next(scalars, keep_a, came_a, keep_b, came_b):
    next_a, next_b = call(
        next_two_kernel,
        scalars,
        (keep_a, came_a, keep_b, came_b),
        [shaped(keep_a.shape[1:], BF16)] * 2,
    )
    last_a = send(next_a, first_axis(3))
    last_b = send(next_b, first_axis(1))
    return keep_a, came_a, last_a, keep_b, came_b, last_b


def both_axes(scalars, student, adaptor):
    keep_a, give_a, keep_b, give_b = student
    came_a = send(give_a, first_axis(1))
    came_b = send(give_b, first_axis(3))
    adapt_keep_a, adapt_came_a, adapt_keep_b, adapt_came_b = adaptor
    adapt_parts = first_next(scalars, adapt_keep_a, adapt_came_a, adapt_keep_b, adapt_came_b)
    keep_b, *adapt_lasts = lax.optimization_barrier((keep_b, adapt_parts[2], adapt_parts[5]))
    parts = first_next(scalars, keep_a, came_a, keep_b, came_b)
    piece = (2, 2, 40, 1280)
    shapes = [shaped(piece, F32), shaped(piece, BF16)]
    scratch = [pltpu.VMEM((8, 40, 1280), F32)]
    keep, give = call(
        functools.partial(axis_two_kernel, 1),
        scalars,
        parts,
        shapes,
        scratch,
    )
    came = send(give, second_axis(1))
    keep, adapt_last = lax.optimization_barrier((keep, adapt_lasts[0]))
    adapt_parts = (*adapt_parts[:2], adapt_last, *adapt_parts[3:5], adapt_lasts[1])
    adapt_keep, adapt_give = call(
        functools.partial(axis_two_kernel, 3), scalars, adapt_parts, shapes, scratch
    )
    adapt_came = send(adapt_give, second_axis(3))
    (onward,) = call(next_kernel, scalars, (keep, came), [shaped(piece[1:], BF16)])
    last = send(onward, second_axis(3))
    onward, adapt_came = lax.optimization_barrier((onward, adapt_came))
    (adapt_next,) = call(
        next_kernel, scalars, (adapt_keep, adapt_came), [shaped(piece[1:], BF16)]
    )
    adapt_last = send(adapt_next, second_axis(1))
    piece = (40, 1280)
    mine, given = call(
        functools.partial(total_kernel, KEEP),
        scalars,
        (keep, came, last),
        [shaped(piece, F32), shaped(piece, BF16)],
        [pltpu.VMEM((2, 40, 1280), F32)],
    )
    came = send(given, beside)
    mine, adapt_last = lax.optimization_barrier((mine, adapt_last))
    adapt_mine, adapt_given = call(
        functools.partial(total_kernel, YL),
        scalars,
        (adapt_keep, adapt_came, adapt_last),
        [shaped(piece, F32), shaped(piece, BF16)],
        [pltpu.VMEM((2, 40, 1280), F32)],
    )
    adapt_came = send(adapt_given, beside)
    came, adapt_mine = lax.optimization_barrier((came, adapt_mine))
    return mine, came, adapt_mine, adapt_came


def block_ids(order, positions, per_image):
    slots = jnp.arange(order.shape[0], dtype=jnp.int32)
    image = jnp.sum(
        jnp.where((positions // per_image)[:, None] == slots[None, :], order[None, :], 0), axis=1
    )
    return image * per_image + positions % per_image


def swap_core(yh, core, z, yl, x):
    return (yh, 1 - core, z, yl, x)


def out_across(yh, core, z, yl, x):
    if yh == 1 and core == 1:
        return (0, core, z, 1 - yl, x)


def exchange_across(yh, core, z, yl, x):
    return (1 - yh, core, z, 1 - yl, x)


def body(acts, block_in, block_out, adapt_in, adapt_out, owner):
    core = lax.axis_index("core")
    group_index = lax.axis_index(GROUP)
    x, yl, z = lax.axis_index("x"), lax.axis_index("yl"), lax.axis_index("z")
    wide_count = lax.axis_size(WIDE)
    token_count = acts.shape[1]
    width = acts.shape[2]
    piece = token_count // wide_count
    half = token_count // 2
    per_image = PATCHES // token_count
    loss_scale = 1.0 / (token_count * wide_count) ** 0.5
    scalars = jnp.stack(
        [
            core,
            1 - lax.axis_index("yh"),
            group_index,
            jnp.minimum(group_index, 2),
            yl,
            jnp.where(lax.axis_index("yh") == 0, 1 - yl, yl),
            jnp.where(core == 0, x, z),
            jnp.where(core == 0, z, x),
        ]
    ).astype(jnp.int32)

    own_order = lax.dynamic_index_in_dim(owner, group_index, 0, keepdims=False)
    positions = jnp.arange(token_count, dtype=jnp.int32) // piece
    wanted = block_ids(owner[3], positions, per_image)
    present = block_ids(own_order, positions, per_image)
    inner = jnp.arange(token_count, dtype=jnp.int32) % piece
    sorter = (wanted[:, None] == present[None, :]) & (inner[:, None] == inner[None, :])
    sorter = sorter.astype(BF16)

    hidden, hand, slope, output, outgoing = block_forward(scalars, acts, block_in, block_out)

    crossed = send(output, out_across)
    handed = send(hand, swap_core)
    hidden_crossed = send(hidden, out_across)
    arrived = lax.all_to_all(outgoing, WIDE, split_axis=0, concat_axis=0, tiled=True)
    (shared,) = call(
        pick_kernel, scalars, (output, crossed), [shaped((token_count, width), BF16)]
    )
    features = send(shared, swap_core)
    student, gamma, mixed = adapt_call(
        adapt_forward_kernel,
        scalars,
        (shared, features),
        adapt_in,
        adapt_out,
        [
            shaped((token_count, width), BF16),
            shaped((token_count, 640), BF16),
            shaped((token_count, width + 640), F32),
        ],
    )
    mixed, handed = lax.optimization_barrier((mixed, handed))
    grad_pred, grad_zeta, kept, given = adapt_call(
        functools.partial(adapt_backward_kernel, loss_scale),
        scalars,
        (sorter, arrived, mixed),
        adapt_in,
        adapt_out,
        [
            shaped((token_count, width), BF16),
            shaped((token_count, 640), BF16),
            shaped((half, width), F32),
            shaped((half, width), BF16),
        ],
    )

    came = send(given, swap_core)
    adapt_keep_a, adapt_give_a, adapt_keep_b, adapt_give_b = call(
        adapt_partial_kernel,
        scalars,
        (student, grad_zeta, gamma, grad_pred),
        [shaped((2, 8, 40, 640), BF16)] * 4,
        [pltpu.VMEM((32, 40, 1280), F32)],
        24,
        4 * token_count * width * 640,
    )
    came, adapt_keep_a = lax.optimization_barrier((came, adapt_keep_a))
    pair, pair_b = call(
        pair_kernel,
        scalars,
        (kept, came),
        [shaped((half, width), F32), shaped((half, width), BF16)],
    )
    pair, hidden_crossed = lax.optimization_barrier((pair, hidden_crossed))
    hidden_core = send(hidden_crossed, swap_core)
    across = send(pair_b, exchange_across)
    left, slopes, weights = stage(
        scalars, (hidden_crossed, hidden_core, hand, handed, slope, block_out)
    )
    across, left = lax.optimization_barrier((across, left))
    adapt_came_a = send(adapt_give_a, first_axis(1))
    adapt_came_b = send(adapt_give_b, first_axis(3))
    (mine,) = call(half_kernel, scalars, (pair, across), [shaped((half, width), BF16)])
    other = send(mine, swap_core)
    other, adapt_came_a, adapt_came_b = lax.optimization_barrier(
        (other, adapt_came_a, adapt_came_b)
    )
    keep_a, give_a, keep_b, give_b = student_partial(
        scalars, (left, slopes, weights), mine, other
    )
    mine, came, adapt_mine, adapt_came = both_axes(
        scalars,
        (keep_a, give_a, keep_b, give_b),
        (adapt_keep_a, adapt_came_a, adapt_keep_b, adapt_came_b),
    )
    piece, piece_b = call(
        piece_kernel, scalars, (mine, came), [shaped((40, 1280), F32), shaped((40, 1280), BF16)]
    )
    out_high = send(piece_b, exchange_across)
    low_piece = send(piece, swap_core)
    out_low = send(out_high, swap_core)
    piece, adapt_came = lax.optimization_barrier((piece, adapt_came))
    grad_first, grad_second = call(
        adapt_last_kernel,
        scalars,
        (adapt_mine, adapt_came),
        [shaped((1, 40, 640), F32), shaped((1, 20, 1280), F32)],
    )
    grad_in_sum, grad_out_sum = call(
        last_kernel,
        scalars,
        (piece, low_piece, out_low, out_high),
        [shaped((1, 40, 2560), F32), shaped((1, 80, 1280), F32)],
    )
    return (grad_first, grad_second, grad_in_sum, grad_out_sum)


def solution(mesh):
    fine = Mesh(mesh.devices.reshape(SIZES), ALL)
    placed = (
        P(GROUP, WIDE, None),
        P(GROUP, None, None),
        P(GROUP, None, None),
        P(),
        P(),
        P(),
    )
    return jax.shard_map(
        body,
        mesh=fine,
        in_specs=placed,
        out_specs=(P(GROUP, WIDE, None),) * 4,
        check_vma=False,
    )
```

```python
import functools

import jax
import jax.numpy as jnp
from jax import lax
from jax.experimental import pallas as pl
from jax.experimental.pallas import tpu as pltpu
from jax.sharding import Mesh
from jax.sharding import PartitionSpec as P

PATCHES = 1024


EPS = 1e-06
WIDE = ("z", "yl", "x")
GROUP = ("yh", "core")
ALL = GROUP + WIDE
SIZES = (2, 2, 4, 2, 4)
MIB = 1024 * 1024
BF16 = jnp.bfloat16


def cost(flops, moved):
    return pl.CostEstimate(flops=flops, bytes_accessed=moved, transcendentals=0)


F32 = jnp.float32
CORE, FLIP, GROUP_AT, CHOSEN, YL, KEEP, FIRST, SECOND = range(8)


def route(move):
    pairs = []
    for flat in range(128):
        x, yl, z, core, yh = flat % 4, flat // 4 % 2, flat // 8 % 4, flat // 32 % 2, flat // 64
        to = move(yh, core, z, yl, x)
        if to is not None:
            yh, core, z, yl, x = to
            pairs.append((flat, (((yh * 2 + core) * 4 + z % 4) * 2 + yl) * 4 + x % 4))
    return pairs


def send(value, move):
    return lax.ppermute(value, ALL, route(move))


def vmem(count):
    return [pl.BlockSpec(memory_space=pltpu.VMEM)] * count


def smem():
    return pl.BlockSpec(memory_space=pltpu.SMEM)


def in_hbm(*weights):
    return [pltpu.with_memory_space_constraint(w, pltpu.HBM) for w in weights]


def shaped(shape, dtype):
    return jax.ShapeDtypeStruct(shape, dtype)


def call(kernel, scalars, inputs, outputs, scratch=(), grant=16, flops=0):
    moved = sum(a.size * a.dtype.itemsize for a in (*inputs, *outputs))
    return pl.pallas_call(
        kernel,
        out_shape=list(outputs),
        in_specs=[smem()] + vmem(len(inputs)),
        out_specs=vmem(len(outputs)),
        scratch_shapes=list(scratch),
        compiler_params=pltpu.CompilerParams(vmem_limit_bytes=grant * MIB),
        cost_estimate=cost(flops, moved),
    )(scalars, *inputs)


def contract_rows(left, right):
    return lax.dot_general(
        left, right, (((0,), (0,)), ((), ())), preferred_element_type=F32
    )


def contract_cols(left, right):
    return lax.dot_general(
        left, right, (((1,), (1,)), ((), ())), preferred_element_type=F32
    )


def gelu_parts(point):
    root = 0.7978845608028654
    square = point * point
    bent = jnp.tanh(root * (point + 0.044715 * point * square))
    share = 0.5 * (1.0 + bent)
    slope = share + 0.5 * point * (1.0 - bent * bent) * (root * (1.0 + 0.134145 * square))
    return point * share, slope


CHUNK = 512


def forward_kernel(
    at, acts_hbm, first_hbm, second_hbm, hidden_hbm, hand_hbm, slope_hbm, out_ref, sent_ref,
    acts_ref, first_ref, second_ref, total, hidden_ref, normed_ref, slope_ref,
    first_sem, second_sem, hidden_sem, slope_sem, other_sem,
):
    tokens, hidden_width = slope_ref.shape
    width = out_ref.shape[1]
    count = hidden_width // CHUNK

    def first_copy(j):
        cut = pl.ds(j * CHUNK, CHUNK)
        return pltpu.make_async_copy(
            first_hbm.at[0, :, cut], first_ref.at[j], first_sem.at[j]
        )

    def second_copy(j):
        cut = pl.ds(j * CHUNK, CHUNK)
        return pltpu.make_async_copy(
            second_hbm.at[0, cut, :], second_ref.at[j], second_sem.at[j]
        )

    def hidden_copy(j):
        cut = pl.ds(j * CHUNK, CHUNK)
        return pltpu.make_async_copy(
            hidden_ref.at[:, cut], hidden_hbm.at[:, cut], hidden_sem.at[j]
        )

    def slope_copy(part):
        cut = pl.ds(part * (hidden_width // 2), hidden_width // 2)
        target = slope_hbm if part else hand_hbm.at[pl.ds(width + tokens, tokens)]
        return pltpu.make_async_copy(slope_ref.at[:, cut], target, slope_sem.at[part])

    def weight_copy(j):
        rows = min(CHUNK, width - j * CHUNK)
        return pltpu.make_async_copy(
            second_ref.at[j, pl.ds(0, rows)],
            hand_hbm.at[pl.ds(j * CHUNK, rows)],
            other_sem.at[2 + j],
        )

    acts_copy = pltpu.make_async_copy(acts_hbm.at[0], acts_ref, other_sem.at[0])
    normed_copy = pltpu.make_async_copy(
        normed_ref, hand_hbm.at[pl.ds(width, tokens)], other_sem.at[1]
    )
    acts_copy.start()
    first_copy(0).start()
    second_copy(0).start()
    first_copy(1).start()
    acts_copy.wait()
    values = acts_ref[...].astype(F32)
    center = values - jnp.mean(values, axis=-1, keepdims=True)
    spread = jnp.mean(center * center, axis=-1, keepdims=True)
    normed = (center * lax.rsqrt(spread + EPS)).astype(BF16)
    normed_ref[...] = normed
    normed_copy.start()
    total[...] = values
    first_copy(0).wait()
    before = jnp.dot(normed, first_ref[0], preferred_element_type=F32)
    for j in range(count):
        if j + 1 < count:
            second_copy(j + 1).start()
        if j + 2 < count:
            first_copy(j + 2).start()
        second_copy(j).wait()
        if j * CHUNK < width:
            weight_copy(j).start()
        if j + 1 < count:
            first_copy(j + 1).wait()
            later = jnp.dot(normed, first_ref[j + 1], preferred_element_type=F32)
        else:
            later = None
        hidden, slope = gelu_parts(before)
        hidden = hidden.astype(BF16)
        slope_ref[:, j * CHUNK : (j + 1) * CHUNK] = slope.astype(BF16)
        hidden_ref[:, j * CHUNK : (j + 1) * CHUNK] = hidden
        hidden_copy(j).start()
        if j == count // 2:
            slope_copy(0).start()
        total[...] += jnp.dot(hidden, second_ref[j], preferred_element_type=F32)
        before = later
    slope_copy(1).start()
    out_ref[...] = total[...].astype(BF16)
    for block in range(8):
        source = jnp.where(at[FLIP] == 1, block ^ 1, block) * 32
        sent_ref[block * 32 : block * 32 + 32] = total[
            pl.ds(pl.multiple_of(source, 32), 32)
        ].astype(BF16)
    for j in range(count):
        hidden_copy(j).wait()
        if j * CHUNK < width:
            weight_copy(j).wait()
    for part in range(2):
        slope_copy(part).wait()
    normed_copy.wait()


def block_forward(scalars, acts, block_in, block_out):
    _, tokens, width = acts.shape
    hidden = block_in.shape[2]
    count = hidden // CHUNK
    return pl.pallas_call(
        forward_kernel,
        out_shape=[
            pltpu.HBM((tokens, hidden), BF16),
            pltpu.HBM((hidden // 2 + 2 * tokens, width), BF16),
            pltpu.HBM((tokens, hidden // 2), BF16),
            shaped((tokens, width), BF16),
            shaped((tokens, width), BF16),
        ],
        in_specs=[smem()] + [pl.BlockSpec(memory_space=pltpu.HBM)] * 3,
        out_specs=[pl.BlockSpec(memory_space=pltpu.HBM)] * 3 + vmem(2),
        scratch_shapes=[
            pltpu.VMEM((tokens, width), BF16),
            pltpu.VMEM((count, width, CHUNK), BF16),
            pltpu.VMEM((count, CHUNK, width), BF16),
            pltpu.VMEM((tokens, width), F32),
            pltpu.VMEM((tokens, hidden), BF16),
            pltpu.VMEM((tokens, width), BF16),
            pltpu.VMEM((tokens, hidden), BF16),
            pltpu.SemaphoreType.DMA((count,)),
            pltpu.SemaphoreType.DMA((count,)),
            pltpu.SemaphoreType.DMA((count,)),
            pltpu.SemaphoreType.DMA((count,)),
            pltpu.SemaphoreType.DMA((2 + count,)),
        ],
        compiler_params=pltpu.CompilerParams(vmem_limit_bytes=32 * MIB),
        cost_estimate=cost(4 * tokens * width * hidden, 16777216),
    )(scalars, *in_hbm(acts, block_in, block_out))


def weight_copies(at, first_hbm, second_hbm, first_ref, second_ref, sems):
    first = pltpu.make_async_copy(first_hbm.at[at[CHOSEN]], first_ref, sems.at[0])
    second = pltpu.make_async_copy(second_hbm.at[at[CHOSEN]], second_ref, sems.at[1])
    return first, second


def pick_kernel(at, own_ref, crossed_ref, shared_ref):
    @pl.when(at[FLIP] == 0)
    def _():
        shared_ref[...] = own_ref[...]

    @pl.when(at[FLIP] == 1)
    def _():
        shared_ref[...] = crossed_ref[...]


def adapt_forward_kernel(
    at, shared_ref, handed_ref, first_hbm, second_hbm,
    student_ref, gamma_ref, mixed_ref, first_ref, second_ref, sems,
):
    first, second = weight_copies(at, first_hbm, second_hbm, first_ref, second_ref, sems)
    first.start()
    second.start()
    for core, source in enumerate((handed_ref, shared_ref)):

        @pl.when(at[CORE] == core)
        def _(source=source):
            student_ref[...] = source[...]

    first.wait()
    zeta = jnp.dot(student_ref[...], first_ref[...], preferred_element_type=F32)
    gamma, slope = gelu_parts(zeta)
    gamma = gamma.astype(BF16)
    gamma_ref[...] = gamma
    mixed_ref[:, 1280:] = slope
    second.wait()
    mixed_ref[:, :1280] = jnp.dot(gamma, second_ref[...], preferred_element_type=F32)


def adapt_call(kernel, scalars, inputs, adapt_in, adapt_out, outputs):
    return pl.pallas_call(
        kernel,
        out_shape=list(outputs),
        in_specs=[smem()] + vmem(len(inputs)) + [pl.BlockSpec(memory_space=pl.ANY)] * 2,
        out_specs=vmem(len(outputs)),
        scratch_shapes=[
            pltpu.VMEM(adapt_in.shape[1:], BF16),
            pltpu.VMEM(adapt_out.shape[1:], BF16),
            pltpu.SemaphoreType.DMA((2,)),
        ],
        compiler_params=pltpu.CompilerParams(vmem_limit_bytes=24 * MIB),
        cost_estimate=cost(1024, 1024),
    )(scalars, *inputs, *in_hbm(adapt_in, adapt_out))


def adapt_backward_kernel(
    scale, at, sorter_ref, arrived_ref, mixed_ref, first_hbm, second_hbm,
    grad_pred_ref, grad_zeta_ref, kept_ref, given_ref, first_ref, second_ref, sems,
):
    first_copy, second_copy = weight_copies(
        at, first_hbm, second_hbm, first_ref, second_ref, sems
    )
    second_copy.start()
    first_copy.start()
    target = jnp.dot(sorter_ref[...], arrived_ref[...], preferred_element_type=F32)
    pred = mixed_ref[:, :1280]
    inner = jnp.mean(pred * target, axis=-1, keepdims=True)
    first = jnp.mean(pred * pred, axis=-1, keepdims=True) + EPS
    second = jnp.mean(target * target, axis=-1, keepdims=True) + EPS
    turn = lax.rsqrt(first * second)
    grad_pred = scale * (2.0 * (pred - target) - turn * (target - (inner / first) * pred))
    grad_pred = grad_pred.astype(BF16)
    grad_pred_ref[...] = grad_pred
    second_copy.wait()
    grad_gamma = contract_cols(grad_pred, second_ref[...])
    grad_zeta = (grad_gamma * mixed_ref[:, 1280:]).astype(BF16)
    grad_zeta_ref[...] = grad_zeta
    first_copy.wait()
    grad = contract_cols(grad_zeta, first_ref[...])
    grad = jnp.where(at[GROUP_AT] < 3, grad, 0.0)

    @pl.when(at[CORE] == 0)
    def _():
        kept_ref[...] = grad[:128]
        given_ref[...] = grad[128:].astype(BF16)

    @pl.when(at[CORE] == 1)
    def _():
        kept_ref[...] = grad[128:]
        given_ref[...] = grad[:128].astype(BF16)


def pair_kernel(at, kept_ref, came_ref, pair_ref, sent_ref):
    pair = kept_ref[...] + came_ref[...].astype(F32)
    pair_ref[...] = pair
    sent_ref[...] = pair.astype(BF16)


def half_kernel(at, pair_ref, across_ref, out_ref):
    out_ref[...] = (pair_ref[...] + across_ref[...].astype(F32)).astype(BF16)


def join_halves(at, mine_ref, other_ref, joined):
    @pl.when(at[CORE] == 0)
    def _():
        joined[:128] = mine_ref[...]
        joined[128:] = other_ref[...]

    @pl.when(at[CORE] == 1)
    def _():
        joined[:128] = other_ref[...]
        joined[128:] = mine_ref[...]


def hand_out(at, terms, turn, keep_ref, give_ref, columns=slice(None)):
    for place in range(8):
        for ref, lines in ((keep_ref, (0, turn ^ 2)), (give_ref, (turn, 2))):
            for slot, mask in enumerate(lines):
                line = at[FIRST] ^ mask
                wide = jnp.where(
                    at[CORE] == 0, place * 4 + line, line * 8 + place % 2 * 4 + place // 2
                )
                ref[slot, place] = terms[wide, :, columns].astype(BF16)


def stage_kernel(
    at, crossed_hbm, crossed_core_hbm, hand_hbm, hand_core_hbm, slope_hbm, second_hbm,
    left, slope, weight, sems,
):
    tokens, width = slope.shape
    weight_part = pl.ds(0, width)
    normed_part, slope_part = pl.ds(width, tokens), pl.ds(width + tokens, tokens)

    def student_copies(normed, slopes, weights):
        copies = (
            pltpu.make_async_copy(normed, left.at[:, pl.ds(0, width)], sems.at[0]),
            pltpu.make_async_copy(slopes, slope, sems.at[1]),
            pltpu.make_async_copy(weights, weight, sems.at[2]),
        )
        for copy in copies:
            copy.start()
        for copy in copies:
            copy.wait()

    for core, source in enumerate((crossed_core_hbm, crossed_hbm)):

        @pl.when((at[FLIP] == 1) & (at[CORE] == core))
        def _(source=source):
            copy = pltpu.make_async_copy(source, left, sems.at[0])
            copy.start()
            copy.wait()

    @pl.when((at[FLIP] == 0) & (at[CORE] == 0))
    def _():
        student_copies(
            hand_core_hbm.at[normed_part],
            hand_core_hbm.at[slope_part],
            hand_core_hbm.at[weight_part],
        )

    @pl.when((at[FLIP] == 0) & (at[CORE] == 1))
    def _():
        student_copies(
            hand_hbm.at[normed_part], slope_hbm, second_hbm.at[0, pl.ds(width, width), :]
        )


def stage(scalars, sources):
    tokens, width = sources[4].shape
    return pl.pallas_call(
        stage_kernel,
        out_shape=[
            shaped((tokens, 2 * width), BF16),
            shaped((tokens, width), BF16),
            shaped((width, width), BF16),
        ],
        in_specs=[smem()] + [pl.BlockSpec(memory_space=pltpu.HBM)] * 6,
        out_specs=vmem(3),
        scratch_shapes=[pltpu.SemaphoreType.DMA((3,))],
        compiler_params=pltpu.CompilerParams(vmem_limit_bytes=16 * MIB),
        cost_estimate=cost(0, 8388608),
    )(scalars, *in_hbm(*sources))


def student_kernel(
    at, left, slope, weight, mine_ref, other_ref, keep_a, give_a, keep_b, give_b, joined, before, terms
):
    join_halves(at, mine_ref, other_ref, joined)

    @pl.when(at[FLIP] == 1)
    def _():
        right = jnp.where(at[CORE] == 0, joined[:, :640], joined[:, 640:])
        for start in range(0, 2560, 640):
            block = contract_rows(left[:, start : start + 640], right)
            for index in range(8):
                row = index * 80
                terms[start // 80 + index, :, :640] = block[row : row + 40].astype(BF16)
                terms[start // 80 + index, :, 640:] = block[row + 40 : row + 80].astype(BF16)

    @pl.when(at[FLIP] == 0)
    def _():
        for start in range(0, 1280, 640):
            cut = slice(start, start + 640)
            grad_hidden = contract_cols(joined[...], weight[cut])
            before[:, cut] = (grad_hidden * slope[:, cut].astype(F32)).astype(BF16)
        for start in range(0, 1280, 640):
            block = contract_rows(left[:, start : start + 640], before[...]).astype(BF16)
            for index in range(16):
                terms[start // 40 + index] = block[index * 40 : index * 40 + 40]

    hand_out(at, terms, 1, keep_a, give_a, slice(0, 640))
    hand_out(at, terms, 3, keep_b, give_b, slice(640, 1280))


def student_partial(scalars, staged, mine, other):
    half, width = mine.shape
    tokens = 2 * half
    return call(
        student_kernel,
        scalars,
        (*staged, mine, other),
        [shaped((2, 8, 40, 640), BF16)] * 4,
        [
            pltpu.VMEM((tokens, width), BF16),
            pltpu.VMEM((tokens, width), BF16),
            pltpu.VMEM((32, 40, 1280), BF16),
        ],
        24,
        4 * tokens * width * width,
    )


def adapt_partial_kernel(
    turn, at, student_ref, grad_zeta_ref, gamma_ref, grad_pred_ref, keep_ref, give_ref, terms
):
    first = contract_rows(student_ref[...], grad_zeta_ref[...])
    second = contract_rows(gamma_ref[...], grad_pred_ref[...])
    for wide in range(32):
        terms[wide, :, :640] = first[wide * 40 : wide * 40 + 40]
        terms[wide, :20, 640:] = second[wide * 20 : wide * 20 + 20, :640]
        terms[wide, 20:, 640:] = second[wide * 20 : wide * 20 + 20, 640:]
    hand_out(at, terms, turn, keep_ref, give_ref)


def next_kernel(at, keep_ref, came_ref, give_ref):
    give_ref[...] = (keep_ref[1].astype(F32) + came_ref[1].astype(F32)).astype(BF16)


def next_two_kernel(at, keep_a, came_a, keep_b, came_b, give_a, give_b):
    give_a[...] = (keep_a[1].astype(F32) + came_a[1].astype(F32)).astype(BF16)
    give_b[...] = (keep_b[1].astype(F32) + came_b[1].astype(F32)).astype(BF16)


def axis_two_kernel(
    turn, at, keep_a, came_a, last_a, keep_b, came_b, last_b, next_keep_ref, next_give_ref, total
):
    total[:, :, :640] = (
        keep_a[0].astype(F32) + came_a[0].astype(F32) + last_a[...].astype(F32)
    )
    total[:, :, 640:] = (
        keep_b[0].astype(F32) + came_b[0].astype(F32) + last_b[...].astype(F32)
    )
    for ref, lines in ((next_keep_ref, (0, turn ^ 2)), (next_give_ref, (turn, 2))):
        for slot, mask in enumerate(lines):
            line = at[SECOND] ^ mask
            for yl in range(2):
                ref[slot, yl] = total[line * 2 + yl].astype(ref.dtype)


def axis_kernel(turn, at, keep_ref, came_ref, last_ref, next_keep_ref, next_give_ref, total):
    total[...] = (
        keep_ref[0].astype(F32) + came_ref[0].astype(F32) + last_ref[...].astype(F32)
    )
    for ref, lines in ((next_keep_ref, (0, turn ^ 2)), (next_give_ref, (turn, 2))):
        for slot, mask in enumerate(lines):
            line = at[SECOND] ^ mask
            for yl in range(2):
                ref[slot, yl] = total[line * 2 + yl].astype(ref.dtype)


def both_kernel(
    at, keep, came, last, adapt_keep, adapt_came, adapt_last, mine_ref, given_ref, total
):
    total[0] = keep[0] + came[0].astype(F32) + last[...].astype(F32)
    total[1] = adapt_keep[0] + adapt_came[0].astype(F32) + adapt_last[...].astype(F32)
    for slot, own in ((0, at[KEEP]), (1, at[YL])):
        mine_ref[slot] = total[slot, own]
        given_ref[slot] = total[slot, 1 - own].astype(BF16)


def piece_kernel(at, mine_ref, beside_ref, piece_ref, sent_ref, first_ref, second_ref):
    piece = mine_ref[0] + beside_ref[0].astype(F32)
    piece_ref[...] = piece
    sent_ref[...] = piece.astype(BF16)
    total = mine_ref[1] + beside_ref[1].astype(F32)
    total = jnp.where(at[GROUP_AT] < 3, total, 0.0)
    first_ref[0] = total[:, :640]
    second_ref[:, 0, :640] = total[:20, 640:]
    second_ref[:, 0, 640:] = total[20:, 640:]


def last_kernel(at, high_ref, low_ref, out_low_ref, out_high_ref, in_ref, out_ref):
    student = at[GROUP_AT] == 3
    in_ref[0, :, :1280] = jnp.where(student, low_ref[...], 0.0)
    in_ref[0, :, 1280:] = jnp.where(student, high_ref[...], 0.0)
    for start, ref in ((0, out_low_ref), (640, out_high_ref)):
        total = jnp.where(student, ref[...].astype(F32), 0.0)
        out_ref[0, :40, start : start + 640] = total[:, :640]
        out_ref[0, 40:, start : start + 640] = total[:, 640:]


def first_axis(mask):
    def to(yh, core, z, yl, x):
        return (yh, core, z, yl, x ^ mask) if core == 0 else (yh, core, z ^ mask, yl, x)

    return to


def second_axis(mask):
    def to(yh, core, z, yl, x):
        return (yh, core, z ^ mask, yl, x) if core == 0 else (yh, core, z, yl, x ^ mask)

    return to


def beside(yh, core, z, yl, x):
    return (yh, core, z, 1 - yl, x)


def both_axes(scalars, keep_a, give_a, keep_b, give_b, adapt_keep, adapt_came):
    came_a = send(give_a, first_axis(1))
    came_b = send(give_b, first_axis(3))
    keep_b, adapt_came = lax.optimization_barrier((keep_b, adapt_came))
    (adapt_next,) = call(
        next_kernel, scalars, (adapt_keep, adapt_came), [shaped(adapt_keep.shape[1:], BF16)]
    )
    adapt_last = send(adapt_next, first_axis(1))
    next_a, next_b = call(
        next_two_kernel,
        scalars,
        (keep_a, came_a, keep_b, came_b),
        [shaped(keep_a.shape[1:], BF16)] * 2,
    )
    last_a = send(next_a, first_axis(3))
    last_b = send(next_b, first_axis(1))
    piece = (2, 2, 40, 1280)
    shapes = [shaped(piece, F32), shaped(piece, BF16)]
    scratch = [pltpu.VMEM((8, 40, 1280), F32)]
    keep, give = call(
        functools.partial(axis_two_kernel, 1),
        scalars,
        (keep_a, came_a, last_a, keep_b, came_b, last_b),
        shapes,
        scratch,
    )
    came = send(give, second_axis(1))
    keep, adapt_last = lax.optimization_barrier((keep, adapt_last))
    adapt_keep, adapt_give = call(
        functools.partial(axis_kernel, 3), scalars, (adapt_keep, adapt_came, adapt_last), shapes, scratch
    )
    adapt_came = send(adapt_give, second_axis(3))
    (onward,) = call(next_kernel, scalars, (keep, came), [shaped(piece[1:], BF16)])
    last = send(onward, second_axis(3))
    onward, adapt_came = lax.optimization_barrier((onward, adapt_came))
    (adapt_next,) = call(
        next_kernel, scalars, (adapt_keep, adapt_came), [shaped(piece[1:], BF16)]
    )
    adapt_last = send(adapt_next, second_axis(1))
    piece = (2, 40, 1280)
    mine, given = call(
        both_kernel,
        scalars,
        (keep, came, last, adapt_keep, adapt_came, adapt_last),
        [shaped(piece, F32), shaped(piece, BF16)],
        [pltpu.VMEM((2, *piece), F32)],
    )
    return mine, send(given, beside)


def block_ids(order, positions, per_image):
    slots = jnp.arange(order.shape[0], dtype=jnp.int32)
    image = jnp.sum(
        jnp.where((positions // per_image)[:, None] == slots[None, :], order[None, :], 0), axis=1
    )
    return image * per_image + positions % per_image


def swap_core(yh, core, z, yl, x):
    return (yh, 1 - core, z, yl, x)


def out_across(yh, core, z, yl, x):
    if yh == 1 and core == 1:
        return (0, core, z, 1 - yl, x)


def exchange_across(yh, core, z, yl, x):
    return (1 - yh, core, z, 1 - yl, x)


def body(acts, block_in, block_out, adapt_in, adapt_out, owner):
    core = lax.axis_index("core")
    group_index = lax.axis_index(GROUP)
    x, yl, z = lax.axis_index("x"), lax.axis_index("yl"), lax.axis_index("z")
    wide_count = lax.axis_size(WIDE)
    token_count = acts.shape[1]
    width = acts.shape[2]
    piece = token_count // wide_count
    half = token_count // 2
    per_image = PATCHES // token_count
    loss_scale = 1.0 / (token_count * wide_count) ** 0.5
    scalars = jnp.stack(
        [
            core,
            1 - lax.axis_index("yh"),
            group_index,
            jnp.minimum(group_index, 2),
            yl,
            jnp.where(lax.axis_index("yh") == 0, 1 - yl, yl),
            jnp.where(core == 0, x, z),
            jnp.where(core == 0, z, x),
        ]
    ).astype(jnp.int32)

    own_order = lax.dynamic_index_in_dim(owner, group_index, 0, keepdims=False)
    positions = jnp.arange(token_count, dtype=jnp.int32) // piece
    wanted = block_ids(owner[3], positions, per_image)
    present = block_ids(own_order, positions, per_image)
    inner = jnp.arange(token_count, dtype=jnp.int32) % piece
    sorter = (wanted[:, None] == present[None, :]) & (inner[:, None] == inner[None, :])
    sorter = sorter.astype(BF16)

    hidden, hand, slope, output, outgoing = block_forward(scalars, acts, block_in, block_out)

    crossed = send(output, out_across)
    handed = send(hand, swap_core)
    hidden_crossed = send(hidden, out_across)
    arrived = lax.all_to_all(outgoing, WIDE, split_axis=0, concat_axis=0, tiled=True)
    (shared,) = call(
        pick_kernel, scalars, (output, crossed), [shaped((token_count, width), BF16)]
    )
    features = send(shared, swap_core)
    student, gamma, mixed = adapt_call(
        adapt_forward_kernel,
        scalars,
        (shared, features),
        adapt_in,
        adapt_out,
        [
            shaped((token_count, width), BF16),
            shaped((token_count, 640), BF16),
            shaped((token_count, width + 640), F32),
        ],
    )
    mixed, handed = lax.optimization_barrier((mixed, handed))
    grad_pred, grad_zeta, kept, given = adapt_call(
        functools.partial(adapt_backward_kernel, loss_scale),
        scalars,
        (sorter, arrived, mixed),
        adapt_in,
        adapt_out,
        [
            shaped((token_count, width), BF16),
            shaped((token_count, 640), BF16),
            shaped((half, width), F32),
            shaped((half, width), BF16),
        ],
    )

    came = send(given, swap_core)
    adapt_keep, adapt_give = call(
        functools.partial(adapt_partial_kernel, 3),
        scalars,
        (student, grad_zeta, gamma, grad_pred),
        [shaped((2, 8, 40, 1280), BF16)] * 2,
        [pltpu.VMEM((32, 40, 1280), F32)],
        24,
        4 * token_count * width * 640,
    )
    came, adapt_keep = lax.optimization_barrier((came, adapt_keep))
    pair, pair_b = call(
        pair_kernel,
        scalars,
        (kept, came),
        [shaped((half, width), F32), shaped((half, width), BF16)],
    )
    pair, hidden_crossed = lax.optimization_barrier((pair, hidden_crossed))
    hidden_core = send(hidden_crossed, swap_core)
    across = send(pair_b, exchange_across)
    left, slopes, weights = stage(
        scalars, (hidden_crossed, hidden_core, hand, handed, slope, block_out)
    )
    across, left = lax.optimization_barrier((across, left))
    adapt_came = send(adapt_give, first_axis(3))
    (mine,) = call(half_kernel, scalars, (pair, across), [shaped((half, width), BF16)])
    other = send(mine, swap_core)
    keep_a, give_a, keep_b, give_b = student_partial(
        scalars, (left, slopes, weights), mine, other
    )
    mine, came = both_axes(scalars, keep_a, give_a, keep_b, give_b, adapt_keep, adapt_came)
    piece, piece_b, grad_first, grad_second = call(
        piece_kernel,
        scalars,
        (mine, came),
        [
            shaped((40, 1280), F32),
            shaped((40, 1280), BF16),
            shaped((1, 40, 640), F32),
            shaped((20, 1, 1280), F32),
        ],
    )
    grad_second = jnp.swapaxes(grad_second, 0, 1)
    out_high = send(piece_b, exchange_across)
    low_piece = send(piece, swap_core)
    out_low = send(out_high, swap_core)
    grad_in_sum, grad_out_sum = call(
        last_kernel,
        scalars,
        (piece, low_piece, out_low, out_high),
        [shaped((1, 40, 2560), F32), shaped((1, 80, 1280), F32)],
    )
    return (grad_first, grad_second, grad_in_sum, grad_out_sum)


def solution(mesh):
    fine = Mesh(mesh.devices.reshape(SIZES), ALL)
    placed = (
        P(GROUP, WIDE, None),
        P(GROUP, None, None),
        P(GROUP, None, None),
        P(),
        P(),
        P(),
    )
    return jax.shard_map(
        body,
        mesh=fine,
        in_specs=placed,
        out_specs=(P(GROUP, WIDE, None),) * 4,
        check_vma=False,
    )
```

```python
import functools

import jax
import jax.numpy as jnp
from jax import lax
from jax.experimental import pallas as pl
from jax.experimental.pallas import tpu as pltpu
from jax.sharding import Mesh
from jax.sharding import PartitionSpec as P

PATCHES = 1024


EPS = 1e-06
WIDE = ("z", "yl", "x")
GROUP = ("yh", "core")
ALL = GROUP + WIDE
SIZES = (2, 2, 4, 2, 4)
MIB = 1024 * 1024
BF16 = jnp.bfloat16


def cost(flops, moved):
    return pl.CostEstimate(flops=flops, bytes_accessed=moved, transcendentals=0)


F32 = jnp.float32
CORE, FLIP, GROUP_AT, CHOSEN, YL, FIRST, SECOND = range(7)


def route(move):
    pairs = []
    for flat in range(128):
        x, yl, z, core, yh = flat % 4, flat // 4 % 2, flat // 8 % 4, flat // 32 % 2, flat // 64
        to = move(yh, core, z, yl, x)
        if to is not None:
            yh, core, z, yl, x = to
            pairs.append((flat, (((yh * 2 + core) * 4 + z % 4) * 2 + yl) * 4 + x % 4))
    return pairs


def send(value, move):
    return lax.ppermute(value, ALL, route(move))


def vmem(count):
    return [pl.BlockSpec(memory_space=pltpu.VMEM)] * count


def smem():
    return pl.BlockSpec(memory_space=pltpu.SMEM)


def in_hbm(*weights):
    return [pltpu.with_memory_space_constraint(w, pltpu.HBM) for w in weights]


def shaped(shape, dtype):
    return jax.ShapeDtypeStruct(shape, dtype)


def call(kernel, scalars, inputs, outputs, scratch=(), grant=16, flops=0):
    moved = sum(a.size * a.dtype.itemsize for a in (*inputs, *outputs))
    return pl.pallas_call(
        kernel,
        out_shape=list(outputs),
        in_specs=[smem()] + vmem(len(inputs)),
        out_specs=vmem(len(outputs)),
        scratch_shapes=list(scratch),
        compiler_params=pltpu.CompilerParams(vmem_limit_bytes=grant * MIB),
        cost_estimate=cost(flops, moved),
    )(scalars, *inputs)


def contract_rows(left, right):
    return lax.dot_general(
        left, right, (((0,), (0,)), ((), ())), preferred_element_type=F32
    )


def contract_cols(left, right):
    return lax.dot_general(
        left, right, (((1,), (1,)), ((), ())), preferred_element_type=F32
    )


def gelu_parts(point):
    root = 0.7978845608028654
    square = point * point
    bent = jnp.tanh(root * (point + 0.044715 * point * square))
    share = 0.5 * (1.0 + bent)
    slope = share + 0.5 * point * (1.0 - bent * bent) * (root * (1.0 + 0.134145 * square))
    return point * share, slope


CHUNK = 512


def forward_kernel(
    at, acts_hbm, first_hbm, second_hbm, hidden_hbm, hand_hbm, slope_hbm, out_ref, sent_ref,
    acts_ref, first_ref, second_ref, total, hidden_ref, normed_ref, slope_ref,
    first_sem, second_sem, hidden_sem, slope_sem, other_sem,
):
    tokens, hidden_width = slope_ref.shape
    width = out_ref.shape[1]
    count = hidden_width // CHUNK

    def first_copy(j):
        cut = pl.ds(j * CHUNK, CHUNK)
        return pltpu.make_async_copy(
            first_hbm.at[0, :, cut], first_ref.at[j], first_sem.at[j]
        )

    def second_copy(j):
        cut = pl.ds(j * CHUNK, CHUNK)
        return pltpu.make_async_copy(
            second_hbm.at[0, cut, :], second_ref.at[j], second_sem.at[j]
        )

    def hidden_copy(j):
        cut = pl.ds(j * CHUNK, CHUNK)
        return pltpu.make_async_copy(
            hidden_ref.at[:, cut], hidden_hbm.at[:, cut], hidden_sem.at[j]
        )

    def slope_copy(part):
        cut = pl.ds(part * (hidden_width // 2), hidden_width // 2)
        target = slope_hbm if part else hand_hbm.at[pl.ds(width + tokens, tokens)]
        return pltpu.make_async_copy(slope_ref.at[:, cut], target, slope_sem.at[part])

    def weight_copy(j):
        rows = min(CHUNK, width - j * CHUNK)
        return pltpu.make_async_copy(
            second_ref.at[j, pl.ds(0, rows)],
            hand_hbm.at[pl.ds(j * CHUNK, rows)],
            other_sem.at[2 + j],
        )

    acts_copy = pltpu.make_async_copy(acts_hbm.at[0], acts_ref, other_sem.at[0])
    normed_copy = pltpu.make_async_copy(
        normed_ref, hand_hbm.at[pl.ds(width, tokens)], other_sem.at[1]
    )
    acts_copy.start()
    first_copy(0).start()
    second_copy(0).start()
    first_copy(1).start()
    acts_copy.wait()
    values = acts_ref[...].astype(F32)
    center = values - jnp.mean(values, axis=-1, keepdims=True)
    spread = jnp.mean(center * center, axis=-1, keepdims=True)
    normed = (center * lax.rsqrt(spread + EPS)).astype(BF16)
    normed_ref[...] = normed
    normed_copy.start()
    total[...] = values
    first_copy(0).wait()
    before = jnp.dot(normed, first_ref[0], preferred_element_type=F32)
    for j in range(count):
        if j + 1 < count:
            second_copy(j + 1).start()
        if j + 2 < count:
            first_copy(j + 2).start()
        second_copy(j).wait()
        if j * CHUNK < width:
            weight_copy(j).start()
        if j + 1 < count:
            first_copy(j + 1).wait()
            later = jnp.dot(normed, first_ref[j + 1], preferred_element_type=F32)
        else:
            later = None
        hidden, slope = gelu_parts(before)
        hidden = hidden.astype(BF16)
        slope_ref[:, j * CHUNK : (j + 1) * CHUNK] = slope.astype(BF16)
        hidden_ref[:, j * CHUNK : (j + 1) * CHUNK] = hidden
        hidden_copy(j).start()
        if j == count // 2:
            slope_copy(0).start()
        total[...] += jnp.dot(hidden, second_ref[j], preferred_element_type=F32)
        before = later
    slope_copy(1).start()
    out_ref[...] = total[...].astype(BF16)
    for block in range(8):
        source = jnp.where(at[FLIP] == 1, block ^ 1, block) * 32
        sent_ref[block * 32 : block * 32 + 32] = total[
            pl.ds(pl.multiple_of(source, 32), 32)
        ].astype(BF16)
    for j in range(count):
        hidden_copy(j).wait()
        if j * CHUNK < width:
            weight_copy(j).wait()
    for part in range(2):
        slope_copy(part).wait()
    normed_copy.wait()


def block_forward(scalars, acts, block_in, block_out):
    _, tokens, width = acts.shape
    hidden = block_in.shape[2]
    count = hidden // CHUNK
    return pl.pallas_call(
        forward_kernel,
        out_shape=[
            pltpu.HBM((tokens, hidden), BF16),
            pltpu.HBM((hidden // 2 + 2 * tokens, width), BF16),
            pltpu.HBM((tokens, hidden // 2), BF16),
            shaped((tokens, width), BF16),
            shaped((tokens, width), BF16),
        ],
        in_specs=[smem()] + [pl.BlockSpec(memory_space=pltpu.HBM)] * 3,
        out_specs=[pl.BlockSpec(memory_space=pltpu.HBM)] * 3 + vmem(2),
        scratch_shapes=[
            pltpu.VMEM((tokens, width), BF16),
            pltpu.VMEM((count, width, CHUNK), BF16),
            pltpu.VMEM((count, CHUNK, width), BF16),
            pltpu.VMEM((tokens, width), F32),
            pltpu.VMEM((tokens, hidden), BF16),
            pltpu.VMEM((tokens, width), BF16),
            pltpu.VMEM((tokens, hidden), BF16),
            pltpu.SemaphoreType.DMA((count,)),
            pltpu.SemaphoreType.DMA((count,)),
            pltpu.SemaphoreType.DMA((count,)),
            pltpu.SemaphoreType.DMA((count,)),
            pltpu.SemaphoreType.DMA((2 + count,)),
        ],
        compiler_params=pltpu.CompilerParams(vmem_limit_bytes=32 * MIB),
        cost_estimate=cost(4 * tokens * width * hidden, 16777216),
    )(scalars, *in_hbm(acts, block_in, block_out))


def weight_copies(at, first_hbm, second_hbm, first_ref, second_ref, sems):
    first = pltpu.make_async_copy(first_hbm.at[at[CHOSEN]], first_ref, sems.at[0])
    second = pltpu.make_async_copy(second_hbm.at[at[CHOSEN]], second_ref, sems.at[1])
    return first, second


def pick_kernel(at, own_ref, crossed_ref, shared_ref):
    @pl.when(at[FLIP] == 0)
    def _():
        shared_ref[...] = own_ref[...]

    @pl.when(at[FLIP] == 1)
    def _():
        shared_ref[...] = crossed_ref[...]


def adapt_forward_kernel(
    at, shared_ref, handed_ref, first_hbm, second_hbm,
    student_ref, gamma_ref, mixed_ref, first_ref, second_ref, sems,
):
    first, second = weight_copies(at, first_hbm, second_hbm, first_ref, second_ref, sems)
    first.start()
    second.start()
    for core, source in enumerate((handed_ref, shared_ref)):

        @pl.when(at[CORE] == core)
        def _(source=source):
            student_ref[...] = source[...]

    first.wait()
    zeta = jnp.dot(student_ref[...], first_ref[...], preferred_element_type=F32)
    gamma, slope = gelu_parts(zeta)
    gamma = gamma.astype(BF16)
    gamma_ref[...] = gamma
    mixed_ref[:, 1280:] = slope
    second.wait()
    mixed_ref[:, :1280] = jnp.dot(gamma, second_ref[...], preferred_element_type=F32)


def adapt_call(kernel, scalars, inputs, adapt_in, adapt_out, outputs):
    return pl.pallas_call(
        kernel,
        out_shape=list(outputs),
        in_specs=[smem()] + vmem(len(inputs)) + [pl.BlockSpec(memory_space=pl.ANY)] * 2,
        out_specs=vmem(len(outputs)),
        scratch_shapes=[
            pltpu.VMEM(adapt_in.shape[1:], BF16),
            pltpu.VMEM(adapt_out.shape[1:], BF16),
            pltpu.SemaphoreType.DMA((2,)),
        ],
        compiler_params=pltpu.CompilerParams(vmem_limit_bytes=24 * MIB),
        cost_estimate=cost(1024, 1024),
    )(scalars, *inputs, *in_hbm(adapt_in, adapt_out))


def adapt_backward_kernel(
    scale, at, sorter_ref, arrived_ref, mixed_ref, first_hbm, second_hbm,
    grad_pred_ref, grad_zeta_ref, kept_ref, given_ref, first_ref, second_ref, sems,
):
    first_copy, second_copy = weight_copies(
        at, first_hbm, second_hbm, first_ref, second_ref, sems
    )
    second_copy.start()
    first_copy.start()
    target = jnp.dot(sorter_ref[...], arrived_ref[...], preferred_element_type=F32)
    pred = mixed_ref[:, :1280]
    inner = jnp.mean(pred * target, axis=-1, keepdims=True)
    first = jnp.mean(pred * pred, axis=-1, keepdims=True) + EPS
    second = jnp.mean(target * target, axis=-1, keepdims=True) + EPS
    turn = lax.rsqrt(first * second)
    grad_pred = scale * (2.0 * (pred - target) - turn * (target - (inner / first) * pred))
    grad_pred = grad_pred.astype(BF16)
    grad_pred_ref[...] = grad_pred
    second_copy.wait()
    grad_gamma = contract_cols(grad_pred, second_ref[...])
    grad_zeta = (grad_gamma * mixed_ref[:, 1280:]).astype(BF16)
    grad_zeta_ref[...] = grad_zeta
    first_copy.wait()
    grad = contract_cols(grad_zeta, first_ref[...])
    grad = jnp.where(at[GROUP_AT] < 3, grad, 0.0)

    @pl.when(at[CORE] == 0)
    def _():
        kept_ref[...] = grad[:128]
        given_ref[...] = grad[128:].astype(BF16)

    @pl.when(at[CORE] == 1)
    def _():
        kept_ref[...] = grad[128:]
        given_ref[...] = grad[:128].astype(BF16)


def pair_kernel(at, kept_ref, came_ref, pair_ref, sent_ref):
    pair = kept_ref[...] + came_ref[...].astype(F32)
    pair_ref[...] = pair
    sent_ref[...] = pair.astype(BF16)


def half_kernel(at, pair_ref, across_ref, out_ref):
    out_ref[...] = (pair_ref[...] + across_ref[...].astype(F32)).astype(BF16)


def join_halves(at, mine_ref, other_ref, joined):
    @pl.when(at[CORE] == 0)
    def _():
        joined[:128] = mine_ref[...]
        joined[128:] = other_ref[...]

    @pl.when(at[CORE] == 1)
    def _():
        joined[:128] = other_ref[...]
        joined[128:] = mine_ref[...]


def hand_out(at, terms, turn, keep_ref, give_ref, columns=slice(None)):
    for place in range(8):
        for ref, lines in ((keep_ref, (0, turn ^ 2)), (give_ref, (turn, 2))):
            for slot, mask in enumerate(lines):
                line = at[FIRST] ^ mask
                wide = jnp.where(
                    at[CORE] == 0, place * 4 + line, line * 8 + place % 2 * 4 + place // 2
                )
                ref[slot, place] = terms[wide, :, columns].astype(BF16)


def stage_kernel(
    at, crossed_hbm, crossed_core_hbm, hand_hbm, hand_core_hbm, slope_hbm, second_hbm,
    left, slope, weight, sems,
):
    tokens, width = slope.shape
    weight_part = pl.ds(0, width)
    normed_part, slope_part = pl.ds(width, tokens), pl.ds(width + tokens, tokens)

    def student_copies(normed, slopes, weights):
        copies = (
            pltpu.make_async_copy(normed, left.at[:, pl.ds(0, width)], sems.at[0]),
            pltpu.make_async_copy(slopes, slope, sems.at[1]),
            pltpu.make_async_copy(weights, weight, sems.at[2]),
        )
        for copy in copies:
            copy.start()
        for copy in copies:
            copy.wait()

    for core, source in enumerate((crossed_core_hbm, crossed_hbm)):

        @pl.when((at[FLIP] == 1) & (at[CORE] == core))
        def _(source=source):
            copy = pltpu.make_async_copy(source, left, sems.at[0])
            copy.start()
            copy.wait()

    @pl.when((at[FLIP] == 0) & (at[CORE] == 0))
    def _():
        student_copies(
            hand_core_hbm.at[normed_part],
            hand_core_hbm.at[slope_part],
            hand_core_hbm.at[weight_part],
        )

    @pl.when((at[FLIP] == 0) & (at[CORE] == 1))
    def _():
        student_copies(
            hand_hbm.at[normed_part], slope_hbm, second_hbm.at[0, pl.ds(width, width), :]
        )


def stage(scalars, sources):
    tokens, width = sources[4].shape
    return pl.pallas_call(
        stage_kernel,
        out_shape=[
            shaped((tokens, 2 * width), BF16),
            shaped((tokens, width), BF16),
            shaped((width, width), BF16),
        ],
        in_specs=[smem()] + [pl.BlockSpec(memory_space=pltpu.HBM)] * 6,
        out_specs=vmem(3),
        scratch_shapes=[pltpu.SemaphoreType.DMA((3,))],
        compiler_params=pltpu.CompilerParams(vmem_limit_bytes=16 * MIB),
        cost_estimate=cost(0, 8388608),
    )(scalars, *in_hbm(*sources))


def student_kernel(
    at, left, slope, weight, mine_ref, other_ref, keep_a, give_a, keep_b, give_b, joined, before, terms
):
    join_halves(at, mine_ref, other_ref, joined)

    @pl.when(at[FLIP] == 1)
    def _():
        right = jnp.where(at[CORE] == 0, joined[:, :640], joined[:, 640:])
        for start in range(0, 2560, 640):
            block = contract_rows(left[:, start : start + 640], right)
            for index in range(8):
                row = index * 80
                terms[start // 80 + index, :, :640] = block[row : row + 40].astype(BF16)
                terms[start // 80 + index, :, 640:] = block[row + 40 : row + 80].astype(BF16)

    @pl.when(at[FLIP] == 0)
    def _():
        for start in range(0, 1280, 640):
            cut = slice(start, start + 640)
            grad_hidden = contract_cols(joined[...], weight[cut])
            before[:, cut] = (grad_hidden * slope[:, cut].astype(F32)).astype(BF16)
        for start in range(0, 1280, 640):
            block = contract_rows(left[:, start : start + 640], before[...]).astype(BF16)
            for index in range(16):
                terms[start // 40 + index] = block[index * 40 : index * 40 + 40]

    hand_out(at, terms, 1, keep_a, give_a, slice(0, 640))
    hand_out(at, terms, 3, keep_b, give_b, slice(640, 1280))


def student_partial(scalars, staged, mine, other):
    half, width = mine.shape
    tokens = 2 * half
    return call(
        student_kernel,
        scalars,
        (*staged, mine, other),
        [shaped((2, 8, 40, 640), BF16)] * 4,
        [
            pltpu.VMEM((tokens, width), BF16),
            pltpu.VMEM((tokens, width), BF16),
            pltpu.VMEM((32, 40, 1280), BF16),
        ],
        24,
        4 * tokens * width * width,
    )


def adapt_partial_kernel(
    turn, at, student_ref, grad_zeta_ref, gamma_ref, grad_pred_ref, keep_ref, give_ref, terms
):
    first = contract_rows(student_ref[...], grad_zeta_ref[...])
    second = contract_rows(gamma_ref[...], grad_pred_ref[...])
    for wide in range(32):
        terms[wide, :, :640] = first[wide * 40 : wide * 40 + 40]
        terms[wide, :20, 640:] = second[wide * 20 : wide * 20 + 20, :640]
        terms[wide, 20:, 640:] = second[wide * 20 : wide * 20 + 20, 640:]
    hand_out(at, terms, turn, keep_ref, give_ref)


def next_kernel(at, keep_ref, came_ref, give_ref):
    give_ref[...] = (keep_ref[1].astype(F32) + came_ref[1].astype(F32)).astype(BF16)


def next_two_kernel(at, keep_a, came_a, keep_b, came_b, give_a, give_b):
    give_a[...] = (keep_a[1].astype(F32) + came_a[1].astype(F32)).astype(BF16)
    give_b[...] = (keep_b[1].astype(F32) + came_b[1].astype(F32)).astype(BF16)


def axis_two_kernel(
    turn, at, keep_a, came_a, last_a, keep_b, came_b, last_b, next_keep_ref, next_give_ref, total
):
    total[:, :, :640] = (
        keep_a[0].astype(F32) + came_a[0].astype(F32) + last_a[...].astype(F32)
    )
    total[:, :, 640:] = (
        keep_b[0].astype(F32) + came_b[0].astype(F32) + last_b[...].astype(F32)
    )
    for ref, lines in ((next_keep_ref, (0, turn ^ 2)), (next_give_ref, (turn, 2))):
        for slot, mask in enumerate(lines):
            line = at[SECOND] ^ mask
            for yl in range(2):
                ref[slot, yl] = total[line * 2 + yl].astype(ref.dtype)


def axis_kernel(turn, at, keep_ref, came_ref, last_ref, next_keep_ref, next_give_ref, total):
    total[...] = (
        keep_ref[0].astype(F32) + came_ref[0].astype(F32) + last_ref[...].astype(F32)
    )
    for ref, lines in ((next_keep_ref, (0, turn ^ 2)), (next_give_ref, (turn, 2))):
        for slot, mask in enumerate(lines):
            line = at[SECOND] ^ mask
            for yl in range(2):
                ref[slot, yl] = total[line * 2 + yl].astype(ref.dtype)


def both_kernel(
    at, keep, came, last, adapt_keep, adapt_came, adapt_last, mine_ref, given_ref, near_ref, far_ref,
    total,
):
    total[0] = keep[0] + came[0].astype(F32) + last[...].astype(F32)
    total[1] = adapt_keep[0] + adapt_came[0].astype(F32) + adapt_last[...].astype(F32)
    for slot in range(2):
        mine_ref[slot] = total[slot, at[YL]]
        given_ref[slot] = total[slot, 1 - at[YL]].astype(BF16)
    near_ref[...] = total[0, 1 - at[YL]].astype(BF16)
    far_ref[...] = total[0, at[YL]].astype(BF16)


def piece_kernel(
    at, mine_ref, beside_ref, near_ref, far_ref, piece_ref, sent_ref, first_ref, second_ref
):
    piece = mine_ref[0] + beside_ref[0].astype(F32)
    piece_ref[0] = piece
    sent_ref[0] = piece.astype(BF16)
    piece = near_ref[...].astype(F32) + far_ref[...].astype(F32)
    piece_ref[1] = piece
    sent_ref[1] = piece.astype(BF16)
    total = mine_ref[1] + beside_ref[1].astype(F32)
    total = jnp.where(at[GROUP_AT] < 3, total, 0.0)
    first_ref[0] = total[:, :640]
    second_ref[:, 0, :640] = total[:20, 640:]
    second_ref[:, 0, 640:] = total[20:, 640:]


def last_kernel(at, high_ref, low_ref, in_ref, out_ref):
    student = at[GROUP_AT] == 3
    for part, ref in enumerate((low_ref, high_ref)):
        total = jnp.where(student, ref[...].astype(F32), 0.0)
        in_ref[0, :, part * 1280 : part * 1280 + 1280] = total[0]
        out_ref[0, :40, part * 640 : part * 640 + 640] = total[1, :, :640]
        out_ref[0, 40:, part * 640 : part * 640 + 640] = total[1, :, 640:]


def first_axis(mask):
    def to(yh, core, z, yl, x):
        return (yh, core, z, yl, x ^ mask) if core == 0 else (yh, core, z ^ mask, yl, x)

    return to


def second_axis(mask):
    def to(yh, core, z, yl, x):
        return (yh, core, z ^ mask, yl, x) if core == 0 else (yh, core, z, yl, x ^ mask)

    return to


def beside(yh, core, z, yl, x):
    return (yh, core, z, 1 - yl, x)


def both_axes(scalars, keep_a, give_a, keep_b, give_b, adapt_keep, adapt_came):
    came_a = send(give_a, first_axis(1))
    came_b = send(give_b, first_axis(3))
    keep_b, adapt_came = lax.optimization_barrier((keep_b, adapt_came))
    (adapt_next,) = call(
        next_kernel, scalars, (adapt_keep, adapt_came), [shaped(adapt_keep.shape[1:], BF16)]
    )
    adapt_last = send(adapt_next, first_axis(1))
    next_a, next_b = call(
        next_two_kernel,
        scalars,
        (keep_a, came_a, keep_b, came_b),
        [shaped(keep_a.shape[1:], BF16)] * 2,
    )
    last_a = send(next_a, first_axis(3))
    last_b = send(next_b, first_axis(1))
    piece = (2, 2, 40, 1280)
    shapes = [shaped(piece, F32), shaped(piece, BF16)]
    scratch = [pltpu.VMEM((8, 40, 1280), F32)]
    keep, give = call(
        functools.partial(axis_two_kernel, 1),
        scalars,
        (keep_a, came_a, last_a, keep_b, came_b, last_b),
        shapes,
        scratch,
    )
    came = send(give, second_axis(1))
    keep, adapt_last = lax.optimization_barrier((keep, adapt_last))
    adapt_keep, adapt_give = call(
        functools.partial(axis_kernel, 3), scalars, (adapt_keep, adapt_came, adapt_last), shapes, scratch
    )
    adapt_came = send(adapt_give, second_axis(3))
    (onward,) = call(next_kernel, scalars, (keep, came), [shaped(piece[1:], BF16)])
    last = send(onward, second_axis(3))
    onward, adapt_came = lax.optimization_barrier((onward, adapt_came))
    (adapt_next,) = call(
        next_kernel, scalars, (adapt_keep, adapt_came), [shaped(piece[1:], BF16)]
    )
    adapt_last = send(adapt_next, second_axis(1))
    piece = (2, 40, 1280)
    mine, given, near, far = call(
        both_kernel,
        scalars,
        (keep, came, last, adapt_keep, adapt_came, adapt_last),
        [shaped(piece, F32), shaped(piece, BF16)] + [shaped(piece[1:], BF16)] * 2,
        [pltpu.VMEM((2, *piece), F32)],
    )
    return mine, send(given, beside), send(near, exchange_across), send(far, exchange_far)


def block_ids(order, positions, per_image):
    slots = jnp.arange(order.shape[0], dtype=jnp.int32)
    image = jnp.sum(
        jnp.where((positions // per_image)[:, None] == slots[None, :], order[None, :], 0), axis=1
    )
    return image * per_image + positions % per_image


def swap_core(yh, core, z, yl, x):
    return (yh, 1 - core, z, yl, x)


def out_across(yh, core, z, yl, x):
    if yh == 1 and core == 1:
        return (0, core, z, 1 - yl, x)


def exchange_far(yh, core, z, yl, x):
    return (1 - yh, core, z, yl, x)


def exchange_across(yh, core, z, yl, x):
    return (1 - yh, core, z, 1 - yl, x)


def body(acts, block_in, block_out, adapt_in, adapt_out, owner):
    core = lax.axis_index("core")
    group_index = lax.axis_index(GROUP)
    x, yl, z = lax.axis_index("x"), lax.axis_index("yl"), lax.axis_index("z")
    wide_count = lax.axis_size(WIDE)
    token_count = acts.shape[1]
    width = acts.shape[2]
    piece = token_count // wide_count
    half = token_count // 2
    per_image = PATCHES // token_count
    loss_scale = 1.0 / (token_count * wide_count) ** 0.5
    scalars = jnp.stack(
        [
            core,
            1 - lax.axis_index("yh"),
            group_index,
            jnp.minimum(group_index, 2),
            yl,
            jnp.where(core == 0, x, z),
            jnp.where(core == 0, z, x),
        ]
    ).astype(jnp.int32)

    own_order = lax.dynamic_index_in_dim(owner, group_index, 0, keepdims=False)
    positions = jnp.arange(token_count, dtype=jnp.int32) // piece
    wanted = block_ids(owner[3], positions, per_image)
    present = block_ids(own_order, positions, per_image)
    inner = jnp.arange(token_count, dtype=jnp.int32) % piece
    sorter = (wanted[:, None] == present[None, :]) & (inner[:, None] == inner[None, :])
    sorter = sorter.astype(BF16)

    hidden, hand, slope, output, outgoing = block_forward(scalars, acts, block_in, block_out)

    crossed = send(output, out_across)
    handed = send(hand, swap_core)
    hidden_crossed = send(hidden, out_across)
    arrived = lax.all_to_all(outgoing, WIDE, split_axis=0, concat_axis=0, tiled=True)
    (shared,) = call(
        pick_kernel, scalars, (output, crossed), [shaped((token_count, width), BF16)]
    )
    features = send(shared, swap_core)
    student, gamma, mixed = adapt_call(
        adapt_forward_kernel,
        scalars,
        (shared, features),
        adapt_in,
        adapt_out,
        [
            shaped((token_count, width), BF16),
            shaped((token_count, 640), BF16),
            shaped((token_count, width + 640), F32),
        ],
    )
    mixed, handed = lax.optimization_barrier((mixed, handed))
    grad_pred, grad_zeta, kept, given = adapt_call(
        functools.partial(adapt_backward_kernel, loss_scale),
        scalars,
        (sorter, arrived, mixed),
        adapt_in,
        adapt_out,
        [
            shaped((token_count, width), BF16),
            shaped((token_count, 640), BF16),
            shaped((half, width), F32),
            shaped((half, width), BF16),
        ],
    )

    came = send(given, swap_core)
    adapt_keep, adapt_give = call(
        functools.partial(adapt_partial_kernel, 3),
        scalars,
        (student, grad_zeta, gamma, grad_pred),
        [shaped((2, 8, 40, 1280), BF16)] * 2,
        [pltpu.VMEM((32, 40, 1280), F32)],
        24,
        4 * token_count * width * 640,
    )
    came, adapt_keep = lax.optimization_barrier((came, adapt_keep))
    pair, pair_b = call(
        pair_kernel,
        scalars,
        (kept, came),
        [shaped((half, width), F32), shaped((half, width), BF16)],
    )
    pair, hidden_crossed = lax.optimization_barrier((pair, hidden_crossed))
    hidden_core = send(hidden_crossed, swap_core)
    across = send(pair_b, exchange_across)
    left, slopes, weights = stage(
        scalars, (hidden_crossed, hidden_core, hand, handed, slope, block_out)
    )
    across, left = lax.optimization_barrier((across, left))
    adapt_came = send(adapt_give, first_axis(3))
    (mine,) = call(half_kernel, scalars, (pair, across), [shaped((half, width), BF16)])
    other = send(mine, swap_core)
    keep_a, give_a, keep_b, give_b = student_partial(
        scalars, (left, slopes, weights), mine, other
    )
    parts = both_axes(scalars, keep_a, give_a, keep_b, give_b, adapt_keep, adapt_came)
    piece, piece_b, grad_first, grad_second = call(
        piece_kernel,
        scalars,
        parts,
        [
            shaped((2, 40, 1280), F32),
            shaped((2, 40, 1280), BF16),
            shaped((1, 40, 640), F32),
            shaped((20, 1, 1280), F32),
        ],
    )
    grad_second = jnp.swapaxes(grad_second, 0, 1)
    grad_in_sum, grad_out_sum = call(
        last_kernel,
        scalars,
        (piece, send(piece_b, swap_core)),
        [shaped((1, 40, 2560), F32), shaped((1, 80, 1280), F32)],
    )
    return (grad_first, grad_second, grad_in_sum, grad_out_sum)


def solution(mesh):
    fine = Mesh(mesh.devices.reshape(SIZES), ALL)
    placed = (
        P(GROUP, WIDE, None),
        P(GROUP, None, None),
        P(GROUP, None, None),
        P(),
        P(),
        P(),
    )
    return jax.shard_map(
        body,
        mesh=fine,
        in_specs=placed,
        out_specs=(P(GROUP, WIDE, None),) * 4,
        check_vma=False,
    )
```

```python
import functools

import jax
import jax.numpy as jnp
from jax import lax
from jax.experimental import pallas as pl
from jax.experimental.pallas import tpu as pltpu
from jax.sharding import Mesh
from jax.sharding import PartitionSpec as P

PATCHES = 1024


EPS = 1e-06
WIDE = ("z", "yl", "x")
GROUP = ("yh", "core")
ALL = GROUP + WIDE
SIZES = (2, 2, 4, 2, 4)
MIB = 1024 * 1024
BF16 = jnp.bfloat16


def cost(flops, moved):
    return pl.CostEstimate(flops=flops, bytes_accessed=moved, transcendentals=0)


F32 = jnp.float32
CORE, FLIP, GROUP_AT, CHOSEN, YL, FIRST, SECOND = range(7)


def route(move):
    pairs = []
    for flat in range(128):
        x, yl, z, core, yh = flat % 4, flat // 4 % 2, flat // 8 % 4, flat // 32 % 2, flat // 64
        to = move(yh, core, z, yl, x)
        if to is not None:
            yh, core, z, yl, x = to
            pairs.append((flat, (((yh * 2 + core) * 4 + z % 4) * 2 + yl) * 4 + x % 4))
    return pairs


def send(value, move):
    return lax.ppermute(value, ALL, route(move))


def vmem(count):
    return [pl.BlockSpec(memory_space=pltpu.VMEM)] * count


def smem():
    return pl.BlockSpec(memory_space=pltpu.SMEM)


def in_hbm(*weights):
    return [pltpu.with_memory_space_constraint(w, pltpu.HBM) for w in weights]


def shaped(shape, dtype):
    return jax.ShapeDtypeStruct(shape, dtype)


def call(kernel, scalars, inputs, outputs, scratch=(), grant=16, flops=0):
    moved = sum(a.size * a.dtype.itemsize for a in (*inputs, *outputs))
    return pl.pallas_call(
        kernel,
        out_shape=list(outputs),
        in_specs=[smem()] + vmem(len(inputs)),
        out_specs=vmem(len(outputs)),
        scratch_shapes=list(scratch),
        compiler_params=pltpu.CompilerParams(vmem_limit_bytes=grant * MIB),
        cost_estimate=cost(flops, moved),
    )(scalars, *inputs)


def contract_rows(left, right):
    return lax.dot_general(
        left, right, (((0,), (0,)), ((), ())), preferred_element_type=F32
    )


def contract_cols(left, right):
    return lax.dot_general(
        left, right, (((1,), (1,)), ((), ())), preferred_element_type=F32
    )


def gelu_parts(point):
    root = 0.7978845608028654
    square = point * point
    bent = jnp.tanh(root * (point + 0.044715 * point * square))
    share = 0.5 * (1.0 + bent)
    slope = share + 0.5 * point * (1.0 - bent * bent) * (root * (1.0 + 0.134145 * square))
    return point * share, slope


CHUNK = 512


def forward_kernel(
    at, acts_hbm, first_hbm, second_hbm, hidden_hbm, hand_hbm, slope_hbm, out_ref, sent_ref,
    acts_ref, first_ref, second_ref, total, hidden_ref, normed_ref, slope_ref,
    first_sem, second_sem, hidden_sem, slope_sem, other_sem,
):
    tokens, hidden_width = slope_ref.shape
    width = out_ref.shape[1]
    count = hidden_width // CHUNK

    def first_copy(j):
        cut = pl.ds(j * CHUNK, CHUNK)
        return pltpu.make_async_copy(
            first_hbm.at[0, :, cut], first_ref.at[j], first_sem.at[j]
        )

    def second_copy(j):
        cut = pl.ds(j * CHUNK, CHUNK)
        return pltpu.make_async_copy(
            second_hbm.at[0, cut, :], second_ref.at[j], second_sem.at[j]
        )

    def hidden_copy(j):
        cut = pl.ds(j * CHUNK, CHUNK)
        return pltpu.make_async_copy(
            hidden_ref.at[:, cut], hidden_hbm.at[:, cut], hidden_sem.at[j]
        )

    def slope_copy(part):
        cut = pl.ds(part * (hidden_width // 2), hidden_width // 2)
        target = slope_hbm if part else hand_hbm.at[pl.ds(width + tokens, tokens)]
        return pltpu.make_async_copy(slope_ref.at[:, cut], target, slope_sem.at[part])

    def weight_copy(j):
        rows = min(CHUNK, width - j * CHUNK)
        return pltpu.make_async_copy(
            second_ref.at[j, pl.ds(0, rows)],
            hand_hbm.at[pl.ds(j * CHUNK, rows)],
            other_sem.at[2 + j],
        )

    acts_copy = pltpu.make_async_copy(acts_hbm.at[0], acts_ref, other_sem.at[0])
    normed_copy = pltpu.make_async_copy(
        normed_ref, hand_hbm.at[pl.ds(width, tokens)], other_sem.at[1]
    )
    acts_copy.start()
    first_copy(0).start()
    second_copy(0).start()
    first_copy(1).start()
    acts_copy.wait()
    values = acts_ref[...].astype(F32)
    center = values - jnp.mean(values, axis=-1, keepdims=True)
    spread = jnp.mean(center * center, axis=-1, keepdims=True)
    normed = (center * lax.rsqrt(spread + EPS)).astype(BF16)
    normed_ref[...] = normed
    normed_copy.start()
    total[...] = values
    first_copy(0).wait()
    before = jnp.dot(normed, first_ref[0], preferred_element_type=F32)
    for j in range(count):
        if j + 1 < count:
            second_copy(j + 1).start()
        if j + 2 < count:
            first_copy(j + 2).start()
        second_copy(j).wait()
        if j * CHUNK < width:
            weight_copy(j).start()
        if j + 1 < count:
            first_copy(j + 1).wait()
            later = jnp.dot(normed, first_ref[j + 1], preferred_element_type=F32)
        else:
            later = None
        hidden, slope = gelu_parts(before)
        hidden = hidden.astype(BF16)
        slope_ref[:, j * CHUNK : (j + 1) * CHUNK] = slope.astype(BF16)
        hidden_ref[:, j * CHUNK : (j + 1) * CHUNK] = hidden
        hidden_copy(j).start()
        if j == count // 2:
            slope_copy(0).start()
        total[...] += jnp.dot(hidden, second_ref[j], preferred_element_type=F32)
        before = later
    slope_copy(1).start()
    out_ref[...] = total[...].astype(BF16)
    for block in range(8):
        source = jnp.where(at[FLIP] == 1, block ^ 1, block) * 32
        sent_ref[block * 32 : block * 32 + 32] = total[
            pl.ds(pl.multiple_of(source, 32), 32)
        ].astype(BF16)
    for j in range(count):
        hidden_copy(j).wait()
        if j * CHUNK < width:
            weight_copy(j).wait()
    for part in range(2):
        slope_copy(part).wait()
    normed_copy.wait()


def block_forward(scalars, acts, block_in, block_out):
    _, tokens, width = acts.shape
    hidden = block_in.shape[2]
    count = hidden // CHUNK
    return pl.pallas_call(
        forward_kernel,
        out_shape=[
            pltpu.HBM((tokens, hidden), BF16),
            pltpu.HBM((hidden // 2 + 2 * tokens, width), BF16),
            pltpu.HBM((tokens, hidden // 2), BF16),
            shaped((tokens, width), BF16),
            shaped((tokens, width), BF16),
        ],
        in_specs=[smem()] + [pl.BlockSpec(memory_space=pltpu.HBM)] * 3,
        out_specs=[pl.BlockSpec(memory_space=pltpu.HBM)] * 3 + vmem(2),
        scratch_shapes=[
            pltpu.VMEM((tokens, width), BF16),
            pltpu.VMEM((count, width, CHUNK), BF16),
            pltpu.VMEM((count, CHUNK, width), BF16),
            pltpu.VMEM((tokens, width), F32),
            pltpu.VMEM((tokens, hidden), BF16),
            pltpu.VMEM((tokens, width), BF16),
            pltpu.VMEM((tokens, hidden), BF16),
            pltpu.SemaphoreType.DMA((count,)),
            pltpu.SemaphoreType.DMA((count,)),
            pltpu.SemaphoreType.DMA((count,)),
            pltpu.SemaphoreType.DMA((count,)),
            pltpu.SemaphoreType.DMA((2 + count,)),
        ],
        compiler_params=pltpu.CompilerParams(vmem_limit_bytes=32 * MIB),
        cost_estimate=cost(4 * tokens * width * hidden, 16777216),
    )(scalars, *in_hbm(acts, block_in, block_out))


def weight_copies(at, first_hbm, second_hbm, first_ref, second_ref, sems):
    first = pltpu.make_async_copy(first_hbm.at[at[CHOSEN]], first_ref, sems.at[0])
    second = pltpu.make_async_copy(second_hbm.at[at[CHOSEN]], second_ref, sems.at[1])
    return first, second


def pick_kernel(at, own_ref, crossed_ref, shared_ref):
    @pl.when(at[FLIP] == 0)
    def _():
        shared_ref[...] = own_ref[...]

    @pl.when(at[FLIP] == 1)
    def _():
        shared_ref[...] = crossed_ref[...]


def adapt_forward_kernel(
    at, shared_ref, handed_ref, first_hbm, second_hbm,
    student_ref, gamma_ref, mixed_ref, first_ref, second_ref, sems,
):
    first, second = weight_copies(at, first_hbm, second_hbm, first_ref, second_ref, sems)
    first.start()
    second.start()
    for core, source in enumerate((handed_ref, shared_ref)):

        @pl.when(at[CORE] == core)
        def _(source=source):
            student_ref[...] = source[...]

    first.wait()
    zeta = jnp.dot(student_ref[...], first_ref[...], preferred_element_type=F32)
    gamma, slope = gelu_parts(zeta)
    gamma = gamma.astype(BF16)
    gamma_ref[...] = gamma
    mixed_ref[:, 1280:] = slope
    second.wait()
    mixed_ref[:, :1280] = jnp.dot(gamma, second_ref[...], preferred_element_type=F32)


def adapt_call(kernel, scalars, inputs, adapt_in, adapt_out, outputs):
    return pl.pallas_call(
        kernel,
        out_shape=list(outputs),
        in_specs=[smem()] + vmem(len(inputs)) + [pl.BlockSpec(memory_space=pl.ANY)] * 2,
        out_specs=vmem(len(outputs)),
        scratch_shapes=[
            pltpu.VMEM(adapt_in.shape[1:], BF16),
            pltpu.VMEM(adapt_out.shape[1:], BF16),
            pltpu.SemaphoreType.DMA((2,)),
        ],
        compiler_params=pltpu.CompilerParams(vmem_limit_bytes=24 * MIB),
        cost_estimate=cost(1024, 1024),
    )(scalars, *inputs, *in_hbm(adapt_in, adapt_out))


def adapt_backward_kernel(
    scale, at, sorter_ref, arrived_ref, mixed_ref, first_hbm, second_hbm,
    grad_pred_ref, grad_zeta_ref, kept_ref, given_ref, first_ref, second_ref, sems,
):
    first_copy, second_copy = weight_copies(
        at, first_hbm, second_hbm, first_ref, second_ref, sems
    )
    second_copy.start()
    first_copy.start()
    target = jnp.dot(sorter_ref[...], arrived_ref[...], preferred_element_type=F32)
    pred = mixed_ref[:, :1280]
    inner = jnp.mean(pred * target, axis=-1, keepdims=True)
    first = jnp.mean(pred * pred, axis=-1, keepdims=True) + EPS
    second = jnp.mean(target * target, axis=-1, keepdims=True) + EPS
    turn = lax.rsqrt(first * second)
    grad_pred = scale * (2.0 * (pred - target) - turn * (target - (inner / first) * pred))
    grad_pred = grad_pred.astype(BF16)
    grad_pred_ref[...] = grad_pred
    second_copy.wait()
    grad_gamma = contract_cols(grad_pred, second_ref[...])
    grad_zeta = (grad_gamma * mixed_ref[:, 1280:]).astype(BF16)
    grad_zeta_ref[...] = grad_zeta
    first_copy.wait()
    grad = contract_cols(grad_zeta, first_ref[...])
    grad = jnp.where(at[GROUP_AT] < 3, grad, 0.0)

    @pl.when(at[CORE] == 0)
    def _():
        kept_ref[...] = grad[:128]
        given_ref[...] = grad[128:].astype(BF16)

    @pl.when(at[CORE] == 1)
    def _():
        kept_ref[...] = grad[128:]
        given_ref[...] = grad[:128].astype(BF16)


def pair_kernel(at, kept_ref, came_ref, pair_ref, sent_ref):
    pair = kept_ref[...] + came_ref[...].astype(F32)
    pair_ref[...] = pair
    sent_ref[...] = pair.astype(BF16)


def half_kernel(at, pair_ref, across_ref, out_ref):
    out_ref[...] = (pair_ref[...] + across_ref[...].astype(F32)).astype(BF16)


def join_halves(at, mine_ref, other_ref, joined):
    @pl.when(at[CORE] == 0)
    def _():
        joined[:128] = mine_ref[...]
        joined[128:] = other_ref[...]

    @pl.when(at[CORE] == 1)
    def _():
        joined[:128] = other_ref[...]
        joined[128:] = mine_ref[...]


def hand_out(at, terms, turn, keep_ref, give_ref, columns=slice(None)):
    for place in range(8):
        for ref, lines in ((keep_ref, (0, turn ^ 2)), (give_ref, (turn, 2))):
            for slot, mask in enumerate(lines):
                line = at[FIRST] ^ mask
                wide = jnp.where(
                    at[CORE] == 0, place * 4 + line, line * 8 + place % 2 * 4 + place // 2
                )
                ref[slot, place] = terms[wide, :, columns].astype(BF16)


def stage_kernel(
    at, crossed_hbm, crossed_core_hbm, hand_hbm, hand_core_hbm, slope_hbm, second_hbm,
    left, slope, weight, sems,
):
    tokens, width = slope.shape
    weight_part = pl.ds(0, width)
    normed_part, slope_part = pl.ds(width, tokens), pl.ds(width + tokens, tokens)

    def student_copies(normed, slopes, weights):
        copies = (
            pltpu.make_async_copy(normed, left.at[:, pl.ds(0, width)], sems.at[0]),
            pltpu.make_async_copy(slopes, slope, sems.at[1]),
            pltpu.make_async_copy(weights, weight, sems.at[2]),
        )
        for copy in copies:
            copy.start()
        for copy in copies:
            copy.wait()

    for core, source in enumerate((crossed_core_hbm, crossed_hbm)):

        @pl.when((at[FLIP] == 1) & (at[CORE] == core))
        def _(source=source):
            copy = pltpu.make_async_copy(source, left, sems.at[0])
            copy.start()
            copy.wait()

    @pl.when((at[FLIP] == 0) & (at[CORE] == 0))
    def _():
        student_copies(
            hand_core_hbm.at[normed_part],
            hand_core_hbm.at[slope_part],
            hand_core_hbm.at[weight_part],
        )

    @pl.when((at[FLIP] == 0) & (at[CORE] == 1))
    def _():
        student_copies(
            hand_hbm.at[normed_part], slope_hbm, second_hbm.at[0, pl.ds(width, width), :]
        )


def stage(scalars, sources):
    tokens, width = sources[4].shape
    return pl.pallas_call(
        stage_kernel,
        out_shape=[
            shaped((tokens, 2 * width), BF16),
            shaped((tokens, width), BF16),
            shaped((width, width), BF16),
        ],
        in_specs=[smem()] + [pl.BlockSpec(memory_space=pltpu.HBM)] * 6,
        out_specs=vmem(3),
        scratch_shapes=[pltpu.SemaphoreType.DMA((3,))],
        compiler_params=pltpu.CompilerParams(vmem_limit_bytes=16 * MIB),
        cost_estimate=cost(0, 8388608),
    )(scalars, *in_hbm(*sources))


def student_kernel(
    at, left, slope, weight, mine_ref, other_ref, keep_a, give_a, keep_b, give_b, joined, before, terms
):
    join_halves(at, mine_ref, other_ref, joined)

    @pl.when(at[FLIP] == 1)
    def _():
        right = jnp.where(at[CORE] == 0, joined[:, :640], joined[:, 640:])
        for start in range(0, 2560, 640):
            block = contract_rows(left[:, start : start + 640], right)
            for index in range(8):
                row = index * 80
                terms[start // 80 + index, :, :640] = block[row : row + 40].astype(BF16)
                terms[start // 80 + index, :, 640:] = block[row + 40 : row + 80].astype(BF16)

    @pl.when(at[FLIP] == 0)
    def _():
        for start in range(0, 1280, 640):
            cut = slice(start, start + 640)
            grad_hidden = contract_cols(joined[...], weight[cut])
            before[:, cut] = (grad_hidden * slope[:, cut].astype(F32)).astype(BF16)
        for start in range(0, 1280, 640):
            block = contract_rows(left[:, start : start + 640], before[...]).astype(BF16)
            for index in range(16):
                terms[start // 40 + index] = block[index * 40 : index * 40 + 40]

    hand_out(at, terms, 1, keep_a, give_a, slice(0, 640))
    hand_out(at, terms, 3, keep_b, give_b, slice(640, 1280))


def student_partial(scalars, staged, mine, other):
    half, width = mine.shape
    tokens = 2 * half
    return call(
        student_kernel,
        scalars,
        (*staged, mine, other),
        [shaped((2, 8, 40, 640), BF16)] * 4,
        [
            pltpu.VMEM((tokens, width), BF16),
            pltpu.VMEM((tokens, width), BF16),
            pltpu.VMEM((32, 40, 1280), BF16),
        ],
        24,
        4 * tokens * width * width,
    )


def adapt_partial_kernel(
    turn, at, student_ref, grad_zeta_ref, gamma_ref, grad_pred_ref, keep_ref, give_ref, terms
):
    first = contract_rows(student_ref[...], grad_zeta_ref[...])
    second = contract_rows(gamma_ref[...], grad_pred_ref[...])
    for wide in range(32):
        terms[wide, :, :640] = first[wide * 40 : wide * 40 + 40]
        terms[wide, :20, 640:] = second[wide * 20 : wide * 20 + 20, :640]
        terms[wide, 20:, 640:] = second[wide * 20 : wide * 20 + 20, 640:]
    hand_out(at, terms, turn, keep_ref, give_ref)


def next_kernel(at, keep_ref, came_ref, give_ref):
    give_ref[...] = (keep_ref[1].astype(F32) + came_ref[1].astype(F32)).astype(BF16)


def next_two_kernel(at, keep_a, came_a, keep_b, came_b, give_a, give_b):
    give_a[...] = (keep_a[1].astype(F32) + came_a[1].astype(F32)).astype(BF16)
    give_b[...] = (keep_b[1].astype(F32) + came_b[1].astype(F32)).astype(BF16)


def axis_two_kernel(
    turn, at, keep_a, came_a, last_a, keep_b, came_b, last_b, next_keep_ref, next_give_ref, total
):
    total[:, :, :640] = (
        keep_a[0].astype(F32) + came_a[0].astype(F32) + last_a[...].astype(F32)
    )
    total[:, :, 640:] = (
        keep_b[0].astype(F32) + came_b[0].astype(F32) + last_b[...].astype(F32)
    )
    for ref, lines in ((next_keep_ref, (0, turn ^ 2)), (next_give_ref, (turn, 2))):
        for slot, mask in enumerate(lines):
            line = at[SECOND] ^ mask
            for yl in range(2):
                ref[slot, yl] = total[line * 2 + yl].astype(ref.dtype)


def axis_kernel(turn, at, keep_ref, came_ref, last_ref, next_keep_ref, next_give_ref, total):
    total[...] = (
        keep_ref[0].astype(F32) + came_ref[0].astype(F32) + last_ref[...].astype(F32)
    )
    for ref, lines in ((next_keep_ref, (0, turn ^ 2)), (next_give_ref, (turn, 2))):
        for slot, mask in enumerate(lines):
            line = at[SECOND] ^ mask
            for yl in range(2):
                ref[slot, yl] = total[line * 2 + yl].astype(ref.dtype)


def total_kernel(at, keep, came, last, mine_ref, given_ref, *refs):
    *sent, total = refs
    total[...] = keep[0] + came[0].astype(F32) + last[...].astype(F32)
    mine_ref[...] = total[at[YL]]
    other = total[1 - at[YL]].astype(BF16)
    given_ref[...] = other
    if sent:
        sent[0][...] = other
        sent[1][...] = total[at[YL]].astype(BF16)


def piece_kernel(at, mine_ref, beside_ref, near_ref, far_ref, piece_ref, sent_ref):
    pieces = (
        mine_ref[...] + beside_ref[...].astype(F32),
        near_ref[...].astype(F32) + far_ref[...].astype(F32),
    )
    for slot, piece in enumerate(pieces):
        piece_ref[slot] = piece
        sent_ref[slot] = piece.astype(BF16)


def adapt_last_kernel(at, mine_ref, beside_ref, first_ref, second_ref):
    total = mine_ref[...] + beside_ref[...].astype(F32)
    total = jnp.where(at[GROUP_AT] < 3, total, 0.0)
    first_ref[0] = total[:, :640]
    second_ref[:, 0, :640] = total[:20, 640:]
    second_ref[:, 0, 640:] = total[20:, 640:]


def last_kernel(at, high_ref, low_ref, in_ref, out_ref):
    student = at[GROUP_AT] == 3
    for part, ref in enumerate((low_ref, high_ref)):
        total = jnp.where(student, ref[...].astype(F32), 0.0)
        in_ref[0, :, part * 1280 : part * 1280 + 1280] = total[0]
        out_ref[0, :40, part * 640 : part * 640 + 640] = total[1, :, :640]
        out_ref[0, 40:, part * 640 : part * 640 + 640] = total[1, :, 640:]


def first_axis(mask):
    def to(yh, core, z, yl, x):
        return (yh, core, z, yl, x ^ mask) if core == 0 else (yh, core, z ^ mask, yl, x)

    return to


def second_axis(mask):
    def to(yh, core, z, yl, x):
        return (yh, core, z ^ mask, yl, x) if core == 0 else (yh, core, z, yl, x ^ mask)

    return to


def beside(yh, core, z, yl, x):
    return (yh, core, z, 1 - yl, x)


def both_axes(scalars, keep_a, give_a, keep_b, give_b, adapt_keep, adapt_came):
    came_a = send(give_a, first_axis(1))
    came_b = send(give_b, first_axis(3))
    keep_b, adapt_came = lax.optimization_barrier((keep_b, adapt_came))
    (adapt_next,) = call(
        next_kernel, scalars, (adapt_keep, adapt_came), [shaped(adapt_keep.shape[1:], BF16)]
    )
    adapt_last = send(adapt_next, first_axis(1))
    next_a, next_b = call(
        next_two_kernel,
        scalars,
        (keep_a, came_a, keep_b, came_b),
        [shaped(keep_a.shape[1:], BF16)] * 2,
    )
    last_a = send(next_a, first_axis(3))
    last_b = send(next_b, first_axis(1))
    piece = (2, 2, 40, 1280)
    shapes = [shaped(piece, F32), shaped(piece, BF16)]
    scratch = [pltpu.VMEM((8, 40, 1280), F32)]
    keep, give = call(
        functools.partial(axis_two_kernel, 1),
        scalars,
        (keep_a, came_a, last_a, keep_b, came_b, last_b),
        shapes,
        scratch,
    )
    came = send(give, second_axis(1))
    keep, adapt_last = lax.optimization_barrier((keep, adapt_last))
    adapt_keep, adapt_give = call(
        functools.partial(axis_kernel, 3), scalars, (adapt_keep, adapt_came, adapt_last), shapes, scratch
    )
    adapt_came = send(adapt_give, second_axis(3))
    (onward,) = call(next_kernel, scalars, (keep, came), [shaped(piece[1:], BF16)])
    last = send(onward, second_axis(3))
    onward, adapt_came = lax.optimization_barrier((onward, adapt_came))
    (adapt_next,) = call(
        next_kernel, scalars, (adapt_keep, adapt_came), [shaped(piece[1:], BF16)]
    )
    adapt_last = send(adapt_next, second_axis(1))
    total = [pltpu.VMEM((2, 40, 1280), F32)]
    whole, rounded = shaped((40, 1280), F32), shaped((40, 1280), BF16)
    mine, given, near, far = call(
        total_kernel, scalars, (keep, came, last), [whole, rounded, rounded, rounded], total
    )
    came, near, far = send(given, beside), send(near, exchange_across), send(far, exchange_far)
    mine, adapt_last = lax.optimization_barrier((mine, adapt_last))
    adapt_mine, adapt_given = call(
        total_kernel, scalars, (adapt_keep, adapt_came, adapt_last), [whole, rounded], total
    )
    adapt_came = send(adapt_given, beside)
    came, adapt_mine = lax.optimization_barrier((came, adapt_mine))
    piece, piece_b = call(
        piece_kernel,
        scalars,
        (mine, came, near, far),
        [shaped((2, 40, 1280), F32), shaped((2, 40, 1280), BF16)],
    )
    piece_b, adapt_came = lax.optimization_barrier((piece_b, adapt_came))
    low = send(piece_b, swap_core)
    grad_first, grad_second = call(
        adapt_last_kernel,
        scalars,
        (adapt_mine, adapt_came),
        [shaped((1, 40, 640), F32), shaped((20, 1, 1280), F32)],
    )
    low, grad_first = lax.optimization_barrier((low, grad_first))
    return piece, low, grad_first, grad_second


def block_ids(order, positions, per_image):
    slots = jnp.arange(order.shape[0], dtype=jnp.int32)
    image = jnp.sum(
        jnp.where((positions // per_image)[:, None] == slots[None, :], order[None, :], 0), axis=1
    )
    return image * per_image + positions % per_image


def swap_core(yh, core, z, yl, x):
    return (yh, 1 - core, z, yl, x)


def out_across(yh, core, z, yl, x):
    if yh == 1 and core == 1:
        return (0, core, z, 1 - yl, x)


def exchange_far(yh, core, z, yl, x):
    return (1 - yh, core, z, yl, x)


def exchange_across(yh, core, z, yl, x):
    return (1 - yh, core, z, 1 - yl, x)


def body(acts, block_in, block_out, adapt_in, adapt_out, owner):
    core = lax.axis_index("core")
    group_index = lax.axis_index(GROUP)
    x, yl, z = lax.axis_index("x"), lax.axis_index("yl"), lax.axis_index("z")
    wide_count = lax.axis_size(WIDE)
    token_count = acts.shape[1]
    width = acts.shape[2]
    piece = token_count // wide_count
    half = token_count // 2
    per_image = PATCHES // token_count
    loss_scale = 1.0 / (token_count * wide_count) ** 0.5
    scalars = jnp.stack(
        [
            core,
            1 - lax.axis_index("yh"),
            group_index,
            jnp.minimum(group_index, 2),
            yl,
            jnp.where(core == 0, x, z),
            jnp.where(core == 0, z, x),
        ]
    ).astype(jnp.int32)

    own_order = lax.dynamic_index_in_dim(owner, group_index, 0, keepdims=False)
    positions = jnp.arange(token_count, dtype=jnp.int32) // piece
    wanted = block_ids(owner[3], positions, per_image)
    present = block_ids(own_order, positions, per_image)
    inner = jnp.arange(token_count, dtype=jnp.int32) % piece
    sorter = (wanted[:, None] == present[None, :]) & (inner[:, None] == inner[None, :])
    sorter = sorter.astype(BF16)

    hidden, hand, slope, output, outgoing = block_forward(scalars, acts, block_in, block_out)

    crossed = send(output, out_across)
    handed = send(hand, swap_core)
    hidden_crossed = send(hidden, out_across)
    arrived = lax.all_to_all(outgoing, WIDE, split_axis=0, concat_axis=0, tiled=True)
    (shared,) = call(
        pick_kernel, scalars, (output, crossed), [shaped((token_count, width), BF16)]
    )
    features = send(shared, swap_core)
    student, gamma, mixed = adapt_call(
        adapt_forward_kernel,
        scalars,
        (shared, features),
        adapt_in,
        adapt_out,
        [
            shaped((token_count, width), BF16),
            shaped((token_count, 640), BF16),
            shaped((token_count, width + 640), F32),
        ],
    )
    mixed, handed = lax.optimization_barrier((mixed, handed))
    grad_pred, grad_zeta, kept, given = adapt_call(
        functools.partial(adapt_backward_kernel, loss_scale),
        scalars,
        (sorter, arrived, mixed),
        adapt_in,
        adapt_out,
        [
            shaped((token_count, width), BF16),
            shaped((token_count, 640), BF16),
            shaped((half, width), F32),
            shaped((half, width), BF16),
        ],
    )

    came = send(given, swap_core)
    adapt_keep, adapt_give = call(
        functools.partial(adapt_partial_kernel, 3),
        scalars,
        (student, grad_zeta, gamma, grad_pred),
        [shaped((2, 8, 40, 1280), BF16)] * 2,
        [pltpu.VMEM((32, 40, 1280), F32)],
        24,
        4 * token_count * width * 640,
    )
    came, adapt_keep = lax.optimization_barrier((came, adapt_keep))
    pair, pair_b = call(
        pair_kernel,
        scalars,
        (kept, came),
        [shaped((half, width), F32), shaped((half, width), BF16)],
    )
    pair, hidden_crossed = lax.optimization_barrier((pair, hidden_crossed))
    hidden_core = send(hidden_crossed, swap_core)
    across = send(pair_b, exchange_across)
    left, slopes, weights = stage(
        scalars, (hidden_crossed, hidden_core, hand, handed, slope, block_out)
    )
    across, left = lax.optimization_barrier((across, left))
    adapt_came = send(adapt_give, first_axis(3))
    (mine,) = call(half_kernel, scalars, (pair, across), [shaped((half, width), BF16)])
    other = send(mine, swap_core)
    keep_a, give_a, keep_b, give_b = student_partial(
        scalars, (left, slopes, weights), mine, other
    )
    piece, low, grad_first, grad_second = both_axes(
        scalars, keep_a, give_a, keep_b, give_b, adapt_keep, adapt_came
    )
    grad_second = jnp.swapaxes(grad_second, 0, 1)
    grad_in_sum, grad_out_sum = call(
        last_kernel,
        scalars,
        (piece, low),
        [shaped((1, 40, 2560), F32), shaped((1, 80, 1280), F32)],
    )
    return (grad_first, grad_second, grad_in_sum, grad_out_sum)


def solution(mesh):
    fine = Mesh(mesh.devices.reshape(SIZES), ALL)
    placed = (
        P(GROUP, WIDE, None),
        P(GROUP, None, None),
        P(GROUP, None, None),
        P(),
        P(),
        P(),
    )
    return jax.shard_map(
        body,
        mesh=fine,
        in_specs=placed,
        out_specs=(P(GROUP, WIDE, None),) * 4,
        check_vma=False,
    )
```

```python
import functools

import jax
import jax.numpy as jnp
from jax import lax
from jax.experimental import pallas as pl
from jax.experimental.pallas import tpu as pltpu
from jax.sharding import Mesh
from jax.sharding import PartitionSpec as P

PATCHES = 1024


EPS = 1e-06
WIDE = ("z", "yl", "x")
GROUP = ("yh", "core")
ALL = GROUP + WIDE
SIZES = (2, 2, 4, 2, 4)
MIB = 1024 * 1024
BF16 = jnp.bfloat16


def cost(flops, moved):
    return pl.CostEstimate(flops=flops, bytes_accessed=moved, transcendentals=0)


F32 = jnp.float32
CORE, FLIP, GROUP_AT, CHOSEN, YL, FIRST, SECOND = range(7)


def route(move):
    pairs = []
    for flat in range(128):
        x, yl, z, core, yh = flat % 4, flat // 4 % 2, flat // 8 % 4, flat // 32 % 2, flat // 64
        to = move(yh, core, z, yl, x)
        if to is not None:
            yh, core, z, yl, x = to
            pairs.append((flat, (((yh * 2 + core) * 4 + z % 4) * 2 + yl) * 4 + x % 4))
    return pairs


def send(value, move):
    return lax.ppermute(value, ALL, route(move))


def vmem(count):
    return [pl.BlockSpec(memory_space=pltpu.VMEM)] * count


def smem():
    return pl.BlockSpec(memory_space=pltpu.SMEM)


def in_hbm(*weights):
    return [pltpu.with_memory_space_constraint(w, pltpu.HBM) for w in weights]


def shaped(shape, dtype):
    return jax.ShapeDtypeStruct(shape, dtype)


def call(kernel, scalars, inputs, outputs, scratch=(), grant=16, flops=0):
    moved = sum(a.size * a.dtype.itemsize for a in (*inputs, *outputs))
    return pl.pallas_call(
        kernel,
        out_shape=list(outputs),
        in_specs=[smem()] + vmem(len(inputs)),
        out_specs=vmem(len(outputs)),
        scratch_shapes=list(scratch),
        compiler_params=pltpu.CompilerParams(vmem_limit_bytes=grant * MIB),
        cost_estimate=cost(flops, moved),
    )(scalars, *inputs)


def contract_rows(left, right):
    return lax.dot_general(
        left, right, (((0,), (0,)), ((), ())), preferred_element_type=F32
    )


def contract_cols(left, right):
    return lax.dot_general(
        left, right, (((1,), (1,)), ((), ())), preferred_element_type=F32
    )


def gelu_parts(point):
    root = 0.7978845608028654
    square = point * point
    bent = jnp.tanh(root * (point + 0.044715 * point * square))
    share = 0.5 * (1.0 + bent)
    slope = share + 0.5 * point * (1.0 - bent * bent) * (root * (1.0 + 0.134145 * square))
    return point * share, slope


CHUNK = 256
AHEAD = 3


def forward_kernel(
    at, acts_hbm, first_hbm, second_hbm, hidden_hbm, hand_hbm, slope_hbm, out_ref, sent_ref,
    acts_ref, first_ref, second_ref, total, hidden_ref, normed_ref, slope_ref,
    first_sem, second_sem, hidden_sem, slope_sem, other_sem,
):
    tokens, hidden_width = slope_ref.shape
    width = out_ref.shape[1]
    count = hidden_width // CHUNK

    def first_copy(j):
        cut = pl.ds(j * CHUNK, CHUNK)
        return pltpu.make_async_copy(
            first_hbm.at[0, :, cut], first_ref.at[j], first_sem.at[j]
        )

    def second_copy(j):
        cut = pl.ds(j * CHUNK, CHUNK)
        return pltpu.make_async_copy(
            second_hbm.at[0, cut, :], second_ref.at[j], second_sem.at[j]
        )

    def hidden_copy(j):
        cut = pl.ds(j * CHUNK, CHUNK)
        return pltpu.make_async_copy(
            hidden_ref.at[:, cut], hidden_hbm.at[:, cut], hidden_sem.at[j]
        )

    def slope_copy(part):
        cut = pl.ds(part * (hidden_width // 2), hidden_width // 2)
        target = slope_hbm if part else hand_hbm.at[pl.ds(width + tokens, tokens)]
        return pltpu.make_async_copy(slope_ref.at[:, cut], target, slope_sem.at[part])

    def weight_copy(j):
        rows = min(CHUNK, width - j * CHUNK)
        return pltpu.make_async_copy(
            second_ref.at[j, pl.ds(0, rows)],
            hand_hbm.at[pl.ds(j * CHUNK, rows)],
            other_sem.at[2 + j],
        )

    acts_copy = pltpu.make_async_copy(acts_hbm.at[0], acts_ref, other_sem.at[0])
    normed_copy = pltpu.make_async_copy(
        normed_ref, hand_hbm.at[pl.ds(width, tokens)], other_sem.at[1]
    )
    acts_copy.start()
    for j in range(AHEAD):
        first_copy(j).start()
        second_copy(j).start()
    acts_copy.wait()
    values = acts_ref[...].astype(F32)
    center = values - jnp.mean(values, axis=-1, keepdims=True)
    spread = jnp.mean(center * center, axis=-1, keepdims=True)
    normed = (center * lax.rsqrt(spread + EPS)).astype(BF16)
    normed_ref[...] = normed
    normed_copy.start()
    total[...] = values
    first_copy(0).wait()
    before = jnp.dot(normed, first_ref[0], preferred_element_type=F32)
    for j in range(count):
        if j + AHEAD < count:
            first_copy(j + AHEAD).start()
            second_copy(j + AHEAD).start()
        second_copy(j).wait()
        if j * CHUNK < width:
            weight_copy(j).start()
        if j + 1 < count:
            first_copy(j + 1).wait()
            later = jnp.dot(normed, first_ref[j + 1], preferred_element_type=F32)
        else:
            later = None
        hidden, slope = gelu_parts(before)
        hidden = hidden.astype(BF16)
        slope_ref[:, j * CHUNK : (j + 1) * CHUNK] = slope.astype(BF16)
        hidden_ref[:, j * CHUNK : (j + 1) * CHUNK] = hidden
        hidden_copy(j).start()
        if j == count // 2:
            slope_copy(0).start()
        total[...] += jnp.dot(hidden, second_ref[j], preferred_element_type=F32)
        before = later
    slope_copy(1).start()
    out_ref[...] = total[...].astype(BF16)
    for block in range(8):
        source = jnp.where(at[FLIP] == 1, block ^ 1, block) * 32
        sent_ref[block * 32 : block * 32 + 32] = total[
            pl.ds(pl.multiple_of(source, 32), 32)
        ].astype(BF16)
    for j in range(count):
        hidden_copy(j).wait()
        if j * CHUNK < width:
            weight_copy(j).wait()
    for part in range(2):
        slope_copy(part).wait()
    normed_copy.wait()


def block_forward(scalars, acts, block_in, block_out):
    _, tokens, width = acts.shape
    hidden = block_in.shape[2]
    count = hidden // CHUNK
    return pl.pallas_call(
        forward_kernel,
        out_shape=[
            pltpu.HBM((tokens, hidden), BF16),
            pltpu.HBM((hidden // 2 + 2 * tokens, width), BF16),
            pltpu.HBM((tokens, hidden // 2), BF16),
            shaped((tokens, width), BF16),
            shaped((tokens, width), BF16),
        ],
        in_specs=[smem()] + [pl.BlockSpec(memory_space=pltpu.HBM)] * 3,
        out_specs=[pl.BlockSpec(memory_space=pltpu.HBM)] * 3 + vmem(2),
        scratch_shapes=[
            pltpu.VMEM((tokens, width), BF16),
            pltpu.VMEM((count, width, CHUNK), BF16),
            pltpu.VMEM((count, CHUNK, width), BF16),
            pltpu.VMEM((tokens, width), F32),
            pltpu.VMEM((tokens, hidden), BF16),
            pltpu.VMEM((tokens, width), BF16),
            pltpu.VMEM((tokens, hidden), BF16),
            pltpu.SemaphoreType.DMA((count,)),
            pltpu.SemaphoreType.DMA((count,)),
            pltpu.SemaphoreType.DMA((count,)),
            pltpu.SemaphoreType.DMA((count,)),
            pltpu.SemaphoreType.DMA((2 + count,)),
        ],
        compiler_params=pltpu.CompilerParams(vmem_limit_bytes=32 * MIB),
        cost_estimate=cost(4 * tokens * width * hidden, 16777216),
    )(scalars, *in_hbm(acts, block_in, block_out))


def weight_copies(at, first_hbm, second_hbm, first_ref, second_ref, sems):
    first = pltpu.make_async_copy(first_hbm.at[at[CHOSEN]], first_ref, sems.at[0])
    second = pltpu.make_async_copy(second_hbm.at[at[CHOSEN]], second_ref, sems.at[1])
    return first, second


def pick_kernel(at, own_ref, crossed_ref, shared_ref):
    @pl.when(at[FLIP] == 0)
    def _():
        shared_ref[...] = own_ref[...]

    @pl.when(at[FLIP] == 1)
    def _():
        shared_ref[...] = crossed_ref[...]


def adapt_forward_kernel(
    at, shared_ref, handed_ref, first_hbm, second_hbm,
    student_ref, gamma_ref, mixed_ref, first_ref, second_ref, sems,
):
    first, second = weight_copies(at, first_hbm, second_hbm, first_ref, second_ref, sems)
    first.start()
    second.start()
    for core, source in enumerate((handed_ref, shared_ref)):

        @pl.when(at[CORE] == core)
        def _(source=source):
            student_ref[...] = source[...]

    first.wait()
    zeta = jnp.dot(student_ref[...], first_ref[...], preferred_element_type=F32)
    gamma, slope = gelu_parts(zeta)
    gamma = gamma.astype(BF16)
    gamma_ref[...] = gamma
    mixed_ref[:, 1280:] = slope
    second.wait()
    mixed_ref[:, :1280] = jnp.dot(gamma, second_ref[...], preferred_element_type=F32)


def adapt_call(kernel, scalars, inputs, adapt_in, adapt_out, outputs):
    return pl.pallas_call(
        kernel,
        out_shape=list(outputs),
        in_specs=[smem()] + vmem(len(inputs)) + [pl.BlockSpec(memory_space=pl.ANY)] * 2,
        out_specs=vmem(len(outputs)),
        scratch_shapes=[
            pltpu.VMEM(adapt_in.shape[1:], BF16),
            pltpu.VMEM(adapt_out.shape[1:], BF16),
            pltpu.SemaphoreType.DMA((2,)),
        ],
        compiler_params=pltpu.CompilerParams(vmem_limit_bytes=24 * MIB),
        cost_estimate=cost(1024, 1024),
    )(scalars, *inputs, *in_hbm(adapt_in, adapt_out))


def adapt_backward_kernel(
    scale, at, sorter_ref, arrived_ref, mixed_ref, first_hbm, second_hbm,
    grad_pred_ref, grad_zeta_ref, kept_ref, given_ref, first_ref, second_ref, sems,
):
    first_copy, second_copy = weight_copies(
        at, first_hbm, second_hbm, first_ref, second_ref, sems
    )
    second_copy.start()
    first_copy.start()
    target = jnp.dot(sorter_ref[...], arrived_ref[...], preferred_element_type=F32)
    pred = mixed_ref[:, :1280]
    inner = jnp.mean(pred * target, axis=-1, keepdims=True)
    first = jnp.mean(pred * pred, axis=-1, keepdims=True) + EPS
    second = jnp.mean(target * target, axis=-1, keepdims=True) + EPS
    turn = lax.rsqrt(first * second)
    grad_pred = scale * (2.0 * (pred - target) - turn * (target - (inner / first) * pred))
    grad_pred = grad_pred.astype(BF16)
    grad_pred_ref[...] = grad_pred
    second_copy.wait()
    grad_gamma = contract_cols(grad_pred, second_ref[...])
    grad_zeta = (grad_gamma * mixed_ref[:, 1280:]).astype(BF16)
    grad_zeta_ref[...] = grad_zeta
    first_copy.wait()
    grad = contract_cols(grad_zeta, first_ref[...])
    grad = jnp.where(at[GROUP_AT] < 3, grad, 0.0)

    @pl.when(at[CORE] == 0)
    def _():
        kept_ref[...] = grad[:128]
        given_ref[...] = grad[128:].astype(BF16)

    @pl.when(at[CORE] == 1)
    def _():
        kept_ref[...] = grad[128:]
        given_ref[...] = grad[:128].astype(BF16)


def pair_kernel(at, kept_ref, came_ref, pair_ref, sent_ref):
    pair = kept_ref[...] + came_ref[...].astype(F32)
    pair_ref[...] = pair
    sent_ref[...] = pair.astype(BF16)


def half_kernel(at, pair_ref, across_ref, out_ref):
    out_ref[...] = (pair_ref[...] + across_ref[...].astype(F32)).astype(BF16)


def join_halves(at, mine_ref, other_ref, joined):
    @pl.when(at[CORE] == 0)
    def _():
        joined[:128] = mine_ref[...]
        joined[128:] = other_ref[...]

    @pl.when(at[CORE] == 1)
    def _():
        joined[:128] = other_ref[...]
        joined[128:] = mine_ref[...]


def hand_out(at, terms, turn, keep_ref, give_ref, columns=slice(None)):
    for place in range(8):
        for ref, lines in ((keep_ref, (0, turn ^ 2)), (give_ref, (turn, 2))):
            for slot, mask in enumerate(lines):
                line = at[FIRST] ^ mask
                wide = jnp.where(
                    at[CORE] == 0, place * 4 + line, line * 8 + place % 2 * 4 + place // 2
                )
                ref[slot, place] = terms[wide, :, columns].astype(BF16)


def stage_kernel(
    at, crossed_hbm, crossed_core_hbm, hand_hbm, hand_core_hbm, slope_hbm, second_hbm,
    left, slope, weight, sems,
):
    tokens, width = slope.shape
    weight_part = pl.ds(0, width)
    normed_part, slope_part = pl.ds(width, tokens), pl.ds(width + tokens, tokens)

    def student_copies(normed, slopes, weights):
        copies = (
            pltpu.make_async_copy(normed, left.at[:, pl.ds(0, width)], sems.at[0]),
            pltpu.make_async_copy(slopes, slope, sems.at[1]),
            pltpu.make_async_copy(weights, weight, sems.at[2]),
        )
        for copy in copies:
            copy.start()
        for copy in copies:
            copy.wait()

    for core, source in enumerate((crossed_core_hbm, crossed_hbm)):

        @pl.when((at[FLIP] == 1) & (at[CORE] == core))
        def _(source=source):
            copy = pltpu.make_async_copy(source, left, sems.at[0])
            copy.start()
            copy.wait()

    @pl.when((at[FLIP] == 0) & (at[CORE] == 0))
    def _():
        student_copies(
            hand_core_hbm.at[normed_part],
            hand_core_hbm.at[slope_part],
            hand_core_hbm.at[weight_part],
        )

    @pl.when((at[FLIP] == 0) & (at[CORE] == 1))
    def _():
        student_copies(
            hand_hbm.at[normed_part], slope_hbm, second_hbm.at[0, pl.ds(width, width), :]
        )


def stage(scalars, sources):
    tokens, width = sources[4].shape
    return pl.pallas_call(
        stage_kernel,
        out_shape=[
            shaped((tokens, 2 * width), BF16),
            shaped((tokens, width), BF16),
            shaped((width, width), BF16),
        ],
        in_specs=[smem()] + [pl.BlockSpec(memory_space=pltpu.HBM)] * 6,
        out_specs=vmem(3),
        scratch_shapes=[pltpu.SemaphoreType.DMA((3,))],
        compiler_params=pltpu.CompilerParams(vmem_limit_bytes=16 * MIB),
        cost_estimate=cost(0, 8388608),
    )(scalars, *in_hbm(*sources))


def student_kernel(
    at, left, slope, weight, mine_ref, other_ref, keep_a, give_a, keep_b, give_b, joined, before, terms
):
    join_halves(at, mine_ref, other_ref, joined)

    @pl.when(at[FLIP] == 1)
    def _():
        right = jnp.where(at[CORE] == 0, joined[:, :640], joined[:, 640:])
        for start in range(0, 2560, 640):
            block = contract_rows(left[:, start : start + 640], right)
            for index in range(8):
                row = index * 80
                terms[start // 80 + index, :, :640] = block[row : row + 40].astype(BF16)
                terms[start // 80 + index, :, 640:] = block[row + 40 : row + 80].astype(BF16)

    @pl.when(at[FLIP] == 0)
    def _():
        for start in range(0, 1280, 640):
            cut = slice(start, start + 640)
            grad_hidden = contract_cols(joined[...], weight[cut])
            before[:, cut] = (grad_hidden * slope[:, cut].astype(F32)).astype(BF16)
        for start in range(0, 1280, 640):
            block = contract_rows(left[:, start : start + 640], before[...]).astype(BF16)
            for index in range(16):
                terms[start // 40 + index] = block[index * 40 : index * 40 + 40]

    hand_out(at, terms, 1, keep_a, give_a, slice(0, 640))
    hand_out(at, terms, 3, keep_b, give_b, slice(640, 1280))


def student_partial(scalars, staged, mine, other):
    half, width = mine.shape
    tokens = 2 * half
    return call(
        student_kernel,
        scalars,
        (*staged, mine, other),
        [shaped((2, 8, 40, 640), BF16)] * 4,
        [
            pltpu.VMEM((tokens, width), BF16),
            pltpu.VMEM((tokens, width), BF16),
            pltpu.VMEM((32, 40, 1280), BF16),
        ],
        24,
        4 * tokens * width * width,
    )


def adapt_partial_kernel(
    turn, at, student_ref, grad_zeta_ref, gamma_ref, grad_pred_ref, keep_ref, give_ref, terms
):
    first = contract_rows(student_ref[...], grad_zeta_ref[...])
    second = contract_rows(gamma_ref[...], grad_pred_ref[...])
    for wide in range(32):
        terms[wide, :, :640] = first[wide * 40 : wide * 40 + 40]
        terms[wide, :20, 640:] = second[wide * 20 : wide * 20 + 20, :640]
        terms[wide, 20:, 640:] = second[wide * 20 : wide * 20 + 20, 640:]
    hand_out(at, terms, turn, keep_ref, give_ref)


def next_kernel(at, keep_ref, came_ref, give_ref):
    give_ref[...] = (keep_ref[1].astype(F32) + came_ref[1].astype(F32)).astype(BF16)


def next_two_kernel(at, keep_a, came_a, keep_b, came_b, give_a, give_b):
    give_a[...] = (keep_a[1].astype(F32) + came_a[1].astype(F32)).astype(BF16)
    give_b[...] = (keep_b[1].astype(F32) + came_b[1].astype(F32)).astype(BF16)


def axis_two_kernel(
    turn, at, keep_a, came_a, last_a, keep_b, came_b, last_b, next_keep_ref, next_give_ref, total
):
    total[:, :, :640] = (
        keep_a[0].astype(F32) + came_a[0].astype(F32) + last_a[...].astype(F32)
    )
    total[:, :, 640:] = (
        keep_b[0].astype(F32) + came_b[0].astype(F32) + last_b[...].astype(F32)
    )
    for ref, lines in ((next_keep_ref, (0, turn ^ 2)), (next_give_ref, (turn, 2))):
        for slot, mask in enumerate(lines):
            line = at[SECOND] ^ mask
            for yl in range(2):
                ref[slot, yl] = total[line * 2 + yl].astype(ref.dtype)


def axis_kernel(turn, at, keep_ref, came_ref, last_ref, next_keep_ref, next_give_ref, total):
    total[...] = (
        keep_ref[0].astype(F32) + came_ref[0].astype(F32) + last_ref[...].astype(F32)
    )
    for ref, lines in ((next_keep_ref, (0, turn ^ 2)), (next_give_ref, (turn, 2))):
        for slot, mask in enumerate(lines):
            line = at[SECOND] ^ mask
            for yl in range(2):
                ref[slot, yl] = total[line * 2 + yl].astype(ref.dtype)


def total_kernel(at, keep, came, last, mine_ref, given_ref, *refs):
    *sent, total = refs
    total[...] = keep[0] + came[0].astype(F32) + last[...].astype(F32)
    mine_ref[...] = total[at[YL]]
    other = total[1 - at[YL]].astype(BF16)
    given_ref[...] = other
    if sent:
        sent[0][...] = other
        sent[1][...] = total[at[YL]].astype(BF16)


def piece_kernel(at, mine_ref, beside_ref, near_ref, far_ref, piece_ref, sent_ref):
    pieces = (
        mine_ref[...] + beside_ref[...].astype(F32),
        near_ref[...].astype(F32) + far_ref[...].astype(F32),
    )
    for slot, piece in enumerate(pieces):
        piece_ref[slot] = piece
        sent_ref[slot] = piece.astype(BF16)


def adapt_last_kernel(at, mine_ref, beside_ref, first_ref, second_ref):
    total = mine_ref[...] + beside_ref[...].astype(F32)
    total = jnp.where(at[GROUP_AT] < 3, total, 0.0)
    first_ref[0] = total[:, :640]
    second_ref[:, 0, :640] = total[:20, 640:]
    second_ref[:, 0, 640:] = total[20:, 640:]


def last_kernel(at, high_ref, low_ref, in_ref, out_ref):
    student = at[GROUP_AT] == 3
    for part, ref in enumerate((low_ref, high_ref)):
        total = jnp.where(student, ref[...].astype(F32), 0.0)
        in_ref[0, :, part * 1280 : part * 1280 + 1280] = total[0]
        out_ref[0, :40, part * 640 : part * 640 + 640] = total[1, :, :640]
        out_ref[0, 40:, part * 640 : part * 640 + 640] = total[1, :, 640:]


def first_axis(mask):
    def to(yh, core, z, yl, x):
        return (yh, core, z, yl, x ^ mask) if core == 0 else (yh, core, z ^ mask, yl, x)

    return to


def second_axis(mask):
    def to(yh, core, z, yl, x):
        return (yh, core, z ^ mask, yl, x) if core == 0 else (yh, core, z, yl, x ^ mask)

    return to


def beside(yh, core, z, yl, x):
    return (yh, core, z, 1 - yl, x)


def both_axes(scalars, keep_a, give_a, keep_b, give_b, adapt_keep, adapt_came):
    came_a = send(give_a, first_axis(1))
    came_b = send(give_b, first_axis(3))
    keep_b, adapt_came = lax.optimization_barrier((keep_b, adapt_came))
    (adapt_next,) = call(
        next_kernel, scalars, (adapt_keep, adapt_came), [shaped(adapt_keep.shape[1:], BF16)]
    )
    adapt_last = send(adapt_next, first_axis(1))
    next_a, next_b = call(
        next_two_kernel,
        scalars,
        (keep_a, came_a, keep_b, came_b),
        [shaped(keep_a.shape[1:], BF16)] * 2,
    )
    last_a = send(next_a, first_axis(3))
    last_b = send(next_b, first_axis(1))
    piece = (2, 2, 40, 1280)
    shapes = [shaped(piece, F32), shaped(piece, BF16)]
    scratch = [pltpu.VMEM((8, 40, 1280), F32)]
    keep, give = call(
        functools.partial(axis_two_kernel, 1),
        scalars,
        (keep_a, came_a, last_a, keep_b, came_b, last_b),
        shapes,
        scratch,
    )
    came = send(give, second_axis(1))
    keep, adapt_last = lax.optimization_barrier((keep, adapt_last))
    adapt_keep, adapt_give = call(
        functools.partial(axis_kernel, 3), scalars, (adapt_keep, adapt_came, adapt_last), shapes, scratch
    )
    adapt_came = send(adapt_give, second_axis(3))
    (onward,) = call(next_kernel, scalars, (keep, came), [shaped(piece[1:], BF16)])
    last = send(onward, second_axis(3))
    onward, adapt_came = lax.optimization_barrier((onward, adapt_came))
    (adapt_next,) = call(
        next_kernel, scalars, (adapt_keep, adapt_came), [shaped(piece[1:], BF16)]
    )
    adapt_last = send(adapt_next, second_axis(1))
    total = [pltpu.VMEM((2, 40, 1280), F32)]
    whole, rounded = shaped((40, 1280), F32), shaped((40, 1280), BF16)
    mine, given, near, far = call(
        total_kernel, scalars, (keep, came, last), [whole, rounded, rounded, rounded], total
    )
    came, near, far = send(given, beside), send(near, exchange_across), send(far, exchange_far)
    mine, adapt_last = lax.optimization_barrier((mine, adapt_last))
    adapt_mine, adapt_given = call(
        total_kernel, scalars, (adapt_keep, adapt_came, adapt_last), [whole, rounded], total
    )
    adapt_came = send(adapt_given, beside)
    came, adapt_mine = lax.optimization_barrier((came, adapt_mine))
    piece, piece_b = call(
        piece_kernel,
        scalars,
        (mine, came, near, far),
        [shaped((2, 40, 1280), F32), shaped((2, 40, 1280), BF16)],
    )
    piece_b, adapt_came = lax.optimization_barrier((piece_b, adapt_came))
    low = send(piece_b, swap_core)
    grad_first, grad_second = call(
        adapt_last_kernel,
        scalars,
        (adapt_mine, adapt_came),
        [shaped((1, 40, 640), F32), shaped((20, 1, 1280), F32)],
    )
    low, grad_first = lax.optimization_barrier((low, grad_first))
    return piece, low, grad_first, grad_second


def block_ids(order, positions, per_image):
    slots = jnp.arange(order.shape[0], dtype=jnp.int32)
    image = jnp.sum(
        jnp.where((positions // per_image)[:, None] == slots[None, :], order[None, :], 0), axis=1
    )
    return image * per_image + positions % per_image


def swap_core(yh, core, z, yl, x):
    return (yh, 1 - core, z, yl, x)


def out_across(yh, core, z, yl, x):
    if yh == 1 and core == 1:
        return (0, core, z, 1 - yl, x)


def exchange_far(yh, core, z, yl, x):
    return (1 - yh, core, z, yl, x)


def exchange_across(yh, core, z, yl, x):
    return (1 - yh, core, z, 1 - yl, x)


def body(acts, block_in, block_out, adapt_in, adapt_out, owner):
    core = lax.axis_index("core")
    group_index = lax.axis_index(GROUP)
    x, yl, z = lax.axis_index("x"), lax.axis_index("yl"), lax.axis_index("z")
    wide_count = lax.axis_size(WIDE)
    token_count = acts.shape[1]
    width = acts.shape[2]
    piece = token_count // wide_count
    half = token_count // 2
    per_image = PATCHES // token_count
    loss_scale = 1.0 / (token_count * wide_count) ** 0.5
    scalars = jnp.stack(
        [
            core,
            1 - lax.axis_index("yh"),
            group_index,
            jnp.minimum(group_index, 2),
            yl,
            jnp.where(core == 0, x, z),
            jnp.where(core == 0, z, x),
        ]
    ).astype(jnp.int32)

    own_order = lax.dynamic_index_in_dim(owner, group_index, 0, keepdims=False)
    positions = jnp.arange(token_count, dtype=jnp.int32) // piece
    wanted = block_ids(owner[3], positions, per_image)
    present = block_ids(own_order, positions, per_image)
    inner = jnp.arange(token_count, dtype=jnp.int32) % piece
    sorter = (wanted[:, None] == present[None, :]) & (inner[:, None] == inner[None, :])
    sorter = sorter.astype(BF16)

    hidden, hand, slope, output, outgoing = block_forward(scalars, acts, block_in, block_out)

    crossed = send(output, out_across)
    handed = send(hand, swap_core)
    hidden_crossed = send(hidden, out_across)
    arrived = lax.all_to_all(outgoing, WIDE, split_axis=0, concat_axis=0, tiled=True)
    (shared,) = call(
        pick_kernel, scalars, (output, crossed), [shaped((token_count, width), BF16)]
    )
    features = send(shared, swap_core)
    student, gamma, mixed = adapt_call(
        adapt_forward_kernel,
        scalars,
        (shared, features),
        adapt_in,
        adapt_out,
        [
            shaped((token_count, width), BF16),
            shaped((token_count, 640), BF16),
            shaped((token_count, width + 640), F32),
        ],
    )
    mixed, handed = lax.optimization_barrier((mixed, handed))
    grad_pred, grad_zeta, kept, given = adapt_call(
        functools.partial(adapt_backward_kernel, loss_scale),
        scalars,
        (sorter, arrived, mixed),
        adapt_in,
        adapt_out,
        [
            shaped((token_count, width), BF16),
            shaped((token_count, 640), BF16),
            shaped((half, width), F32),
            shaped((half, width), BF16),
        ],
    )

    came = send(given, swap_core)
    adapt_keep, adapt_give = call(
        functools.partial(adapt_partial_kernel, 3),
        scalars,
        (student, grad_zeta, gamma, grad_pred),
        [shaped((2, 8, 40, 1280), BF16)] * 2,
        [pltpu.VMEM((32, 40, 1280), F32)],
        24,
        4 * token_count * width * 640,
    )
    came, adapt_keep = lax.optimization_barrier((came, adapt_keep))
    pair, pair_b = call(
        pair_kernel,
        scalars,
        (kept, came),
        [shaped((half, width), F32), shaped((half, width), BF16)],
    )
    pair, hidden_crossed = lax.optimization_barrier((pair, hidden_crossed))
    hidden_core = send(hidden_crossed, swap_core)
    across = send(pair_b, exchange_across)
    left, slopes, weights = stage(
        scalars, (hidden_crossed, hidden_core, hand, handed, slope, block_out)
    )
    across, left = lax.optimization_barrier((across, left))
    adapt_came = send(adapt_give, first_axis(3))
    (mine,) = call(half_kernel, scalars, (pair, across), [shaped((half, width), BF16)])
    other = send(mine, swap_core)
    keep_a, give_a, keep_b, give_b = student_partial(
        scalars, (left, slopes, weights), mine, other
    )
    piece, low, grad_first, grad_second = both_axes(
        scalars, keep_a, give_a, keep_b, give_b, adapt_keep, adapt_came
    )
    grad_second = jnp.swapaxes(grad_second, 0, 1)
    grad_in_sum, grad_out_sum = call(
        last_kernel,
        scalars,
        (piece, low),
        [shaped((1, 40, 2560), F32), shaped((1, 80, 1280), F32)],
    )
    return (grad_first, grad_second, grad_in_sum, grad_out_sum)


def solution(mesh):
    fine = Mesh(mesh.devices.reshape(SIZES), ALL)
    placed = (
        P(GROUP, WIDE, None),
        P(GROUP, None, None),
        P(GROUP, None, None),
        P(),
        P(),
        P(),
    )
    return jax.shard_map(
        body,
        mesh=fine,
        in_specs=placed,
        out_specs=(P(GROUP, WIDE, None),) * 4,
        check_vma=False,
    )
```

```python
import functools

import jax
import jax.numpy as jnp
from jax import lax
from jax.experimental import pallas as pl
from jax.experimental.pallas import tpu as pltpu
from jax.sharding import Mesh
from jax.sharding import PartitionSpec as P

PATCHES = 1024


EPS = 1e-06
WIDE = ("z", "yl", "x")
GROUP = ("yh", "core")
ALL = GROUP + WIDE
SIZES = (2, 2, 4, 2, 4)
MIB = 1024 * 1024
BF16 = jnp.bfloat16


def cost(flops, moved):
    return pl.CostEstimate(flops=flops, bytes_accessed=moved, transcendentals=0)


F32 = jnp.float32
CORE, FLIP, GROUP_AT, CHOSEN, YL, FIRST, SECOND = range(7)


def route(move):
    pairs = []
    for flat in range(128):
        x, yl, z, core, yh = flat % 4, flat // 4 % 2, flat // 8 % 4, flat // 32 % 2, flat // 64
        to = move(yh, core, z, yl, x)
        if to is not None:
            yh, core, z, yl, x = to
            pairs.append((flat, (((yh * 2 + core) * 4 + z % 4) * 2 + yl) * 4 + x % 4))
    return pairs


def send(value, move):
    return lax.ppermute(value, ALL, route(move))


def vmem(count):
    return [pl.BlockSpec(memory_space=pltpu.VMEM)] * count


def smem():
    return pl.BlockSpec(memory_space=pltpu.SMEM)


def in_hbm(*weights):
    return [pltpu.with_memory_space_constraint(w, pltpu.HBM) for w in weights]


def shaped(shape, dtype):
    return jax.ShapeDtypeStruct(shape, dtype)


def call(kernel, scalars, inputs, outputs, scratch=(), grant=16, flops=0):
    moved = sum(a.size * a.dtype.itemsize for a in (*inputs, *outputs))
    return pl.pallas_call(
        kernel,
        out_shape=list(outputs),
        in_specs=[smem()] + vmem(len(inputs)),
        out_specs=vmem(len(outputs)),
        scratch_shapes=list(scratch),
        compiler_params=pltpu.CompilerParams(vmem_limit_bytes=grant * MIB),
        cost_estimate=cost(flops, moved),
    )(scalars, *inputs)


def contract_rows(left, right):
    return lax.dot_general(
        left, right, (((0,), (0,)), ((), ())), preferred_element_type=F32
    )


def contract_cols(left, right):
    return lax.dot_general(
        left, right, (((1,), (1,)), ((), ())), preferred_element_type=F32
    )


def gelu_parts(point):
    root = 0.7978845608028654
    square = point * point
    bent = jnp.tanh(root * (point + 0.044715 * point * square))
    share = 0.5 * (1.0 + bent)
    slope = share + 0.5 * point * (1.0 - bent * bent) * (root * (1.0 + 0.134145 * square))
    return point * share, slope


CHUNK = 512


def forward_kernel(
    at, acts_hbm, first_hbm, second_hbm, hidden_hbm, hand_hbm, slope_hbm, out_ref, sent_ref,
    acts_ref, first_ref, second_ref, total, hidden_ref, normed_ref, slope_ref,
    first_sem, second_sem, hidden_sem, slope_sem, other_sem,
):
    tokens, hidden_width = slope_ref.shape
    width = out_ref.shape[1]
    count = hidden_width // CHUNK

    def first_copy(j):
        cut = pl.ds(j * CHUNK, CHUNK)
        return pltpu.make_async_copy(
            first_hbm.at[0, :, cut], first_ref.at[j], first_sem.at[j]
        )

    def second_copy(j):
        cut = pl.ds(j * CHUNK, CHUNK)
        return pltpu.make_async_copy(
            second_hbm.at[0, cut, :], second_ref.at[j], second_sem.at[j]
        )

    def hidden_copy(j):
        cut = pl.ds(j * CHUNK, CHUNK)
        return pltpu.make_async_copy(
            hidden_ref.at[:, cut], hidden_hbm.at[:, cut], hidden_sem.at[j]
        )

    def slope_copy(part):
        cut = pl.ds(part * (hidden_width // 2), hidden_width // 2)
        target = slope_hbm if part else hand_hbm.at[pl.ds(width + tokens, tokens)]
        return pltpu.make_async_copy(slope_ref.at[:, cut], target, slope_sem.at[part])

    def weight_copy(j):
        rows = min(CHUNK, width - j * CHUNK)
        return pltpu.make_async_copy(
            second_ref.at[j, pl.ds(0, rows)],
            hand_hbm.at[pl.ds(j * CHUNK, rows)],
            other_sem.at[2 + j],
        )

    acts_copy = pltpu.make_async_copy(acts_hbm.at[0], acts_ref, other_sem.at[0])
    normed_copy = pltpu.make_async_copy(
        normed_ref, hand_hbm.at[pl.ds(width, tokens)], other_sem.at[1]
    )
    acts_copy.start()
    first_copy(0).start()
    second_copy(0).start()
    first_copy(1).start()
    acts_copy.wait()
    values = acts_ref[...].astype(F32)
    center = values - jnp.mean(values, axis=-1, keepdims=True)
    spread = jnp.mean(center * center, axis=-1, keepdims=True)
    normed = (center * lax.rsqrt(spread + EPS)).astype(BF16)
    normed_ref[...] = normed
    normed_copy.start()
    total[...] = values
    first_copy(0).wait()
    before = jnp.dot(normed, first_ref[0], preferred_element_type=F32)
    for j in range(count):
        if j + 1 < count:
            second_copy(j + 1).start()
        if j + 2 < count:
            first_copy(j + 2).start()
        second_copy(j).wait()
        if j * CHUNK < width:
            weight_copy(j).start()
        if j + 1 < count:
            first_copy(j + 1).wait()
            later = jnp.dot(normed, first_ref[j + 1], preferred_element_type=F32)
        else:
            later = None
        hidden, slope = gelu_parts(before)
        hidden = hidden.astype(BF16)
        slope_ref[:, j * CHUNK : (j + 1) * CHUNK] = slope.astype(BF16)
        hidden_ref[:, j * CHUNK : (j + 1) * CHUNK] = hidden
        hidden_copy(j).start()
        if j == count // 2:
            slope_copy(0).start()
        total[...] += jnp.dot(hidden, second_ref[j], preferred_element_type=F32)
        before = later
    slope_copy(1).start()
    out_ref[...] = total[...].astype(BF16)
    for block in range(8):
        source = jnp.where(at[FLIP] == 1, block ^ 1, block) * 32
        sent_ref[block * 32 : block * 32 + 32] = total[
            pl.ds(pl.multiple_of(source, 32), 32)
        ].astype(BF16)
    for j in range(count):
        hidden_copy(j).wait()
        if j * CHUNK < width:
            weight_copy(j).wait()
    for part in range(2):
        slope_copy(part).wait()
    normed_copy.wait()


def block_forward(scalars, acts, block_in, block_out):
    _, tokens, width = acts.shape
    hidden = block_in.shape[2]
    count = hidden // CHUNK
    return pl.pallas_call(
        forward_kernel,
        out_shape=[
            pltpu.HBM((tokens, hidden), BF16),
            pltpu.HBM((hidden // 2 + 2 * tokens, width), BF16),
            pltpu.HBM((tokens, hidden // 2), BF16),
            shaped((tokens, width), BF16),
            shaped((tokens, width), BF16),
        ],
        in_specs=[smem()] + [pl.BlockSpec(memory_space=pltpu.HBM)] * 3,
        out_specs=[pl.BlockSpec(memory_space=pltpu.HBM)] * 3 + vmem(2),
        scratch_shapes=[
            pltpu.VMEM((tokens, width), BF16),
            pltpu.VMEM((count, width, CHUNK), BF16),
            pltpu.VMEM((count, CHUNK, width), BF16),
            pltpu.VMEM((tokens, width), F32),
            pltpu.VMEM((tokens, hidden), BF16),
            pltpu.VMEM((tokens, width), BF16),
            pltpu.VMEM((tokens, hidden), BF16),
            pltpu.SemaphoreType.DMA((count,)),
            pltpu.SemaphoreType.DMA((count,)),
            pltpu.SemaphoreType.DMA((count,)),
            pltpu.SemaphoreType.DMA((count,)),
            pltpu.SemaphoreType.DMA((2 + count,)),
        ],
        compiler_params=pltpu.CompilerParams(vmem_limit_bytes=32 * MIB),
        cost_estimate=cost(4 * tokens * width * hidden, 16777216),
    )(scalars, *in_hbm(acts, block_in, block_out))


def weight_copies(at, first_hbm, second_hbm, first_ref, second_ref, sems):
    first = pltpu.make_async_copy(first_hbm.at[at[CHOSEN]], first_ref, sems.at[0])
    second = pltpu.make_async_copy(second_hbm.at[at[CHOSEN]], second_ref, sems.at[1])
    return first, second


def pick_kernel(at, own_ref, crossed_ref, shared_ref):
    @pl.when(at[FLIP] == 0)
    def _():
        shared_ref[...] = own_ref[...]

    @pl.when(at[FLIP] == 1)
    def _():
        shared_ref[...] = crossed_ref[...]


def adapt_forward_kernel(
    at, shared_ref, handed_ref, first_hbm, second_hbm,
    student_ref, gamma_ref, mixed_ref, first_ref, second_ref, sems,
):
    first, second = weight_copies(at, first_hbm, second_hbm, first_ref, second_ref, sems)
    first.start()
    second.start()
    for core, source in enumerate((handed_ref, shared_ref)):

        @pl.when(at[CORE] == core)
        def _(source=source):
            student_ref[...] = source[...]

    first.wait()
    zeta = jnp.dot(student_ref[...], first_ref[...], preferred_element_type=F32)
    gamma, slope = gelu_parts(zeta)
    gamma = gamma.astype(BF16)
    gamma_ref[...] = gamma
    mixed_ref[:, 1280:] = slope
    second.wait()
    mixed_ref[:, :1280] = jnp.dot(gamma, second_ref[...], preferred_element_type=F32)


def adapt_call(kernel, scalars, inputs, adapt_in, adapt_out, outputs):
    return pl.pallas_call(
        kernel,
        out_shape=list(outputs),
        in_specs=[smem()] + vmem(len(inputs)) + [pl.BlockSpec(memory_space=pl.ANY)] * 2,
        out_specs=vmem(len(outputs)),
        scratch_shapes=[pltpu.SemaphoreType.DMA((2,))],
        compiler_params=pltpu.CompilerParams(vmem_limit_bytes=24 * MIB),
        cost_estimate=cost(1024, 1024),
    )(scalars, *inputs, *in_hbm(adapt_in, adapt_out))


def adapt_backward_kernel(
    scale, at, sorter_ref, arrived_ref, mixed_ref, first_ref, second_ref,
    grad_pred_ref, grad_zeta_ref, kept_ref, given_ref,
):
    target = jnp.dot(sorter_ref[...], arrived_ref[...], preferred_element_type=F32)
    pred = mixed_ref[:, :1280]
    inner = jnp.mean(pred * target, axis=-1, keepdims=True)
    first = jnp.mean(pred * pred, axis=-1, keepdims=True) + EPS
    second = jnp.mean(target * target, axis=-1, keepdims=True) + EPS
    turn = lax.rsqrt(first * second)
    grad_pred = scale * (2.0 * (pred - target) - turn * (target - (inner / first) * pred))
    grad_pred = grad_pred.astype(BF16)
    grad_pred_ref[...] = grad_pred
    grad_gamma = contract_cols(grad_pred, second_ref[...])
    grad_zeta = (grad_gamma * mixed_ref[:, 1280:]).astype(BF16)
    grad_zeta_ref[...] = grad_zeta
    grad = contract_cols(grad_zeta, first_ref[...])
    grad = jnp.where(at[GROUP_AT] < 3, grad, 0.0)

    @pl.when(at[CORE] == 0)
    def _():
        kept_ref[...] = grad[:128]
        given_ref[...] = grad[128:].astype(BF16)

    @pl.when(at[CORE] == 1)
    def _():
        kept_ref[...] = grad[128:]
        given_ref[...] = grad[:128].astype(BF16)


def pair_kernel(at, kept_ref, came_ref, pair_ref, sent_ref):
    pair = kept_ref[...] + came_ref[...].astype(F32)
    pair_ref[...] = pair
    sent_ref[...] = pair.astype(BF16)


def half_kernel(at, pair_ref, across_ref, out_ref):
    out_ref[...] = (pair_ref[...] + across_ref[...].astype(F32)).astype(BF16)


def join_halves(at, mine_ref, other_ref, joined):
    @pl.when(at[CORE] == 0)
    def _():
        joined[:128] = mine_ref[...]
        joined[128:] = other_ref[...]

    @pl.when(at[CORE] == 1)
    def _():
        joined[:128] = other_ref[...]
        joined[128:] = mine_ref[...]


def hand_out(at, terms, turn, keep_ref, give_ref, columns=slice(None)):
    for place in range(8):
        for ref, lines in ((keep_ref, (0, turn ^ 2)), (give_ref, (turn, 2))):
            for slot, mask in enumerate(lines):
                line = at[FIRST] ^ mask
                wide = jnp.where(
                    at[CORE] == 0, place * 4 + line, line * 8 + place % 2 * 4 + place // 2
                )
                ref[slot, place] = terms[wide, :, columns].astype(BF16)


def stage_kernel(
    at, crossed_hbm, crossed_core_hbm, hand_hbm, hand_core_hbm, slope_hbm, second_hbm,
    left, slope, weight, sems,
):
    tokens, width = slope.shape
    weight_part = pl.ds(0, width)
    normed_part, slope_part = pl.ds(width, tokens), pl.ds(width + tokens, tokens)

    def student_copies(normed, slopes, weights):
        copies = (
            pltpu.make_async_copy(normed, left.at[:, pl.ds(0, width)], sems.at[0]),
            pltpu.make_async_copy(slopes, slope, sems.at[1]),
            pltpu.make_async_copy(weights, weight, sems.at[2]),
        )
        for copy in copies:
            copy.start()
        for copy in copies:
            copy.wait()

    for core, source in enumerate((crossed_core_hbm, crossed_hbm)):

        @pl.when((at[FLIP] == 1) & (at[CORE] == core))
        def _(source=source):
            copy = pltpu.make_async_copy(source, left, sems.at[0])
            copy.start()
            copy.wait()

    @pl.when((at[FLIP] == 0) & (at[CORE] == 0))
    def _():
        student_copies(
            hand_core_hbm.at[normed_part],
            hand_core_hbm.at[slope_part],
            hand_core_hbm.at[weight_part],
        )

    @pl.when((at[FLIP] == 0) & (at[CORE] == 1))
    def _():
        student_copies(
            hand_hbm.at[normed_part], slope_hbm, second_hbm.at[0, pl.ds(width, width), :]
        )


def stage(scalars, sources):
    tokens, width = sources[4].shape
    return pl.pallas_call(
        stage_kernel,
        out_shape=[
            shaped((tokens, 2 * width), BF16),
            shaped((tokens, width), BF16),
            shaped((width, width), BF16),
        ],
        in_specs=[smem()] + [pl.BlockSpec(memory_space=pltpu.HBM)] * 6,
        out_specs=vmem(3),
        scratch_shapes=[pltpu.SemaphoreType.DMA((3,))],
        compiler_params=pltpu.CompilerParams(vmem_limit_bytes=16 * MIB),
        cost_estimate=cost(0, 8388608),
    )(scalars, *in_hbm(*sources))


def student_kernel(
    at, left, slope, weight, mine_ref, other_ref, keep_a, give_a, keep_b, give_b, joined, before, terms
):
    join_halves(at, mine_ref, other_ref, joined)

    @pl.when(at[FLIP] == 1)
    def _():
        right = jnp.where(at[CORE] == 0, joined[:, :640], joined[:, 640:])
        for start in range(0, 2560, 640):
            block = contract_rows(left[:, start : start + 640], right)
            for index in range(8):
                row = index * 80
                terms[start // 80 + index, :, :640] = block[row : row + 40].astype(BF16)
                terms[start // 80 + index, :, 640:] = block[row + 40 : row + 80].astype(BF16)

    @pl.when(at[FLIP] == 0)
    def _():
        for start in range(0, 1280, 640):
            cut = slice(start, start + 640)
            grad_hidden = contract_cols(joined[...], weight[cut])
            before[:, cut] = (grad_hidden * slope[:, cut].astype(F32)).astype(BF16)
        for start in range(0, 1280, 640):
            block = contract_rows(left[:, start : start + 640], before[...]).astype(BF16)
            for index in range(16):
                terms[start // 40 + index] = block[index * 40 : index * 40 + 40]

    hand_out(at, terms, 1, keep_a, give_a, slice(0, 640))
    hand_out(at, terms, 3, keep_b, give_b, slice(640, 1280))


def student_partial(scalars, staged, mine, other):
    half, width = mine.shape
    tokens = 2 * half
    return call(
        student_kernel,
        scalars,
        (*staged, mine, other),
        [shaped((2, 8, 40, 640), BF16)] * 4,
        [
            pltpu.VMEM((tokens, width), BF16),
            pltpu.VMEM((tokens, width), BF16),
            pltpu.VMEM((32, 40, 1280), BF16),
        ],
        24,
        4 * tokens * width * width,
    )


def adapt_partial_kernel(
    turn, at, student_ref, grad_zeta_ref, gamma_ref, grad_pred_ref, keep_ref, give_ref, terms
):
    first = contract_rows(student_ref[...], grad_zeta_ref[...])
    second = contract_rows(gamma_ref[...], grad_pred_ref[...])
    for wide in range(32):
        terms[wide, :, :640] = first[wide * 40 : wide * 40 + 40]
        terms[wide, :20, 640:] = second[wide * 20 : wide * 20 + 20, :640]
        terms[wide, 20:, 640:] = second[wide * 20 : wide * 20 + 20, 640:]
    hand_out(at, terms, turn, keep_ref, give_ref)


def next_kernel(at, keep_ref, came_ref, give_ref):
    give_ref[...] = (keep_ref[1].astype(F32) + came_ref[1].astype(F32)).astype(BF16)


def next_two_kernel(at, keep_a, came_a, keep_b, came_b, give_a, give_b):
    give_a[...] = (keep_a[1].astype(F32) + came_a[1].astype(F32)).astype(BF16)
    give_b[...] = (keep_b[1].astype(F32) + came_b[1].astype(F32)).astype(BF16)


def axis_two_kernel(
    turn, at, keep_a, came_a, last_a, keep_b, came_b, last_b, next_keep_ref, next_give_ref, total
):
    total[:, :, :640] = (
        keep_a[0].astype(F32) + came_a[0].astype(F32) + last_a[...].astype(F32)
    )
    total[:, :, 640:] = (
        keep_b[0].astype(F32) + came_b[0].astype(F32) + last_b[...].astype(F32)
    )
    for ref, lines in ((next_keep_ref, (0, turn ^ 2)), (next_give_ref, (turn, 2))):
        for slot, mask in enumerate(lines):
            line = at[SECOND] ^ mask
            for yl in range(2):
                ref[slot, yl] = total[line * 2 + yl].astype(ref.dtype)


def axis_kernel(turn, at, keep_ref, came_ref, last_ref, next_keep_ref, next_give_ref, total):
    total[...] = (
        keep_ref[0].astype(F32) + came_ref[0].astype(F32) + last_ref[...].astype(F32)
    )
    for ref, lines in ((next_keep_ref, (0, turn ^ 2)), (next_give_ref, (turn, 2))):
        for slot, mask in enumerate(lines):
            line = at[SECOND] ^ mask
            for yl in range(2):
                ref[slot, yl] = total[line * 2 + yl].astype(ref.dtype)


def total_kernel(at, keep, came, last, mine_ref, given_ref, *refs):
    *sent, total = refs
    total[...] = keep[0] + came[0].astype(F32) + last[...].astype(F32)
    mine_ref[...] = total[at[YL]]
    other = total[1 - at[YL]].astype(BF16)
    given_ref[...] = other
    if sent:
        sent[0][...] = other
        sent[1][...] = total[at[YL]].astype(BF16)


def piece_kernel(at, mine_ref, beside_ref, near_ref, far_ref, piece_ref, sent_ref):
    pieces = (
        mine_ref[...] + beside_ref[...].astype(F32),
        near_ref[...].astype(F32) + far_ref[...].astype(F32),
    )
    for slot, piece in enumerate(pieces):
        piece_ref[slot] = piece
        sent_ref[slot] = piece.astype(BF16)


def adapt_last_kernel(at, mine_ref, beside_ref, first_ref, second_ref):
    total = mine_ref[...] + beside_ref[...].astype(F32)
    total = jnp.where(at[GROUP_AT] < 3, total, 0.0)
    first_ref[0] = total[:, :640]
    second_ref[:, 0, :640] = total[:20, 640:]
    second_ref[:, 0, 640:] = total[20:, 640:]


def last_kernel(at, high_ref, low_ref, in_ref, out_ref):
    student = at[GROUP_AT] == 3
    for part, ref in enumerate((low_ref, high_ref)):
        total = jnp.where(student, ref[...].astype(F32), 0.0)
        in_ref[0, :, part * 1280 : part * 1280 + 1280] = total[0]
        out_ref[0, :40, part * 640 : part * 640 + 640] = total[1, :, :640]
        out_ref[0, 40:, part * 640 : part * 640 + 640] = total[1, :, 640:]


def first_axis(mask):
    def to(yh, core, z, yl, x):
        return (yh, core, z, yl, x ^ mask) if core == 0 else (yh, core, z ^ mask, yl, x)

    return to


def second_axis(mask):
    def to(yh, core, z, yl, x):
        return (yh, core, z ^ mask, yl, x) if core == 0 else (yh, core, z, yl, x ^ mask)

    return to


def beside(yh, core, z, yl, x):
    return (yh, core, z, 1 - yl, x)


def both_axes(scalars, keep_a, give_a, keep_b, give_b, adapt_keep, adapt_came):
    came_a = send(give_a, first_axis(1))
    came_b = send(give_b, first_axis(3))
    keep_b, adapt_came = lax.optimization_barrier((keep_b, adapt_came))
    (adapt_next,) = call(
        next_kernel, scalars, (adapt_keep, adapt_came), [shaped(adapt_keep.shape[1:], BF16)]
    )
    adapt_last = send(adapt_next, first_axis(1))
    next_a, next_b = call(
        next_two_kernel,
        scalars,
        (keep_a, came_a, keep_b, came_b),
        [shaped(keep_a.shape[1:], BF16)] * 2,
    )
    last_a = send(next_a, first_axis(3))
    last_b = send(next_b, first_axis(1))
    piece = (2, 2, 40, 1280)
    shapes = [shaped(piece, F32), shaped(piece, BF16)]
    scratch = [pltpu.VMEM((8, 40, 1280), F32)]
    keep, give = call(
        functools.partial(axis_two_kernel, 1),
        scalars,
        (keep_a, came_a, last_a, keep_b, came_b, last_b),
        shapes,
        scratch,
    )
    came = send(give, second_axis(1))
    keep, adapt_last = lax.optimization_barrier((keep, adapt_last))
    adapt_keep, adapt_give = call(
        functools.partial(axis_kernel, 3), scalars, (adapt_keep, adapt_came, adapt_last), shapes, scratch
    )
    adapt_came = send(adapt_give, second_axis(3))
    (onward,) = call(next_kernel, scalars, (keep, came), [shaped(piece[1:], BF16)])
    last = send(onward, second_axis(3))
    onward, adapt_came = lax.optimization_barrier((onward, adapt_came))
    (adapt_next,) = call(
        next_kernel, scalars, (adapt_keep, adapt_came), [shaped(piece[1:], BF16)]
    )
    adapt_last = send(adapt_next, second_axis(1))
    total = [pltpu.VMEM((2, 40, 1280), F32)]
    whole, rounded = shaped((40, 1280), F32), shaped((40, 1280), BF16)
    mine, given, near, far = call(
        total_kernel, scalars, (keep, came, last), [whole, rounded, rounded, rounded], total
    )
    came, near, far = send(given, beside), send(near, exchange_across), send(far, exchange_far)
    mine, adapt_last = lax.optimization_barrier((mine, adapt_last))
    adapt_mine, adapt_given = call(
        total_kernel, scalars, (adapt_keep, adapt_came, adapt_last), [whole, rounded], total
    )
    adapt_came = send(adapt_given, beside)
    came, adapt_mine = lax.optimization_barrier((came, adapt_mine))
    piece, piece_b = call(
        piece_kernel,
        scalars,
        (mine, came, near, far),
        [shaped((2, 40, 1280), F32), shaped((2, 40, 1280), BF16)],
    )
    piece_b, adapt_came = lax.optimization_barrier((piece_b, adapt_came))
    low = send(piece_b, swap_core)
    grad_first, grad_second = call(
        adapt_last_kernel,
        scalars,
        (adapt_mine, adapt_came),
        [shaped((1, 40, 640), F32), shaped((20, 1, 1280), F32)],
    )
    low, grad_first = lax.optimization_barrier((low, grad_first))
    return piece, low, grad_first, grad_second


def block_ids(order, positions, per_image):
    slots = jnp.arange(order.shape[0], dtype=jnp.int32)
    image = jnp.sum(
        jnp.where((positions // per_image)[:, None] == slots[None, :], order[None, :], 0), axis=1
    )
    return image * per_image + positions % per_image


def swap_core(yh, core, z, yl, x):
    return (yh, 1 - core, z, yl, x)


def out_across(yh, core, z, yl, x):
    if yh == 1 and core == 1:
        return (0, core, z, 1 - yl, x)


def exchange_far(yh, core, z, yl, x):
    return (1 - yh, core, z, yl, x)


def exchange_across(yh, core, z, yl, x):
    return (1 - yh, core, z, 1 - yl, x)


def body(acts, block_in, block_out, adapt_in, adapt_out, owner):
    core = lax.axis_index("core")
    group_index = lax.axis_index(GROUP)
    x, yl, z = lax.axis_index("x"), lax.axis_index("yl"), lax.axis_index("z")
    wide_count = lax.axis_size(WIDE)
    token_count = acts.shape[1]
    width = acts.shape[2]
    piece = token_count // wide_count
    half = token_count // 2
    per_image = PATCHES // token_count
    loss_scale = 1.0 / (token_count * wide_count) ** 0.5
    scalars = jnp.stack(
        [
            core,
            1 - lax.axis_index("yh"),
            group_index,
            jnp.minimum(group_index, 2),
            yl,
            jnp.where(core == 0, x, z),
            jnp.where(core == 0, z, x),
        ]
    ).astype(jnp.int32)

    own_order = lax.dynamic_index_in_dim(owner, group_index, 0, keepdims=False)
    positions = jnp.arange(token_count, dtype=jnp.int32) // piece
    wanted = block_ids(owner[3], positions, per_image)
    present = block_ids(own_order, positions, per_image)
    inner = jnp.arange(token_count, dtype=jnp.int32) % piece
    sorter = (wanted[:, None] == present[None, :]) & (inner[:, None] == inner[None, :])
    sorter = sorter.astype(BF16)

    hidden, hand, slope, output, outgoing = block_forward(scalars, acts, block_in, block_out)

    crossed = send(output, out_across)
    handed = send(hand, swap_core)
    hidden_crossed = send(hidden, out_across)
    arrived = lax.all_to_all(outgoing, WIDE, split_axis=0, concat_axis=0, tiled=True)
    (shared,) = call(
        pick_kernel, scalars, (output, crossed), [shaped((token_count, width), BF16)]
    )
    features = send(shared, swap_core)
    student, gamma, mixed, first, second = adapt_call(
        adapt_forward_kernel,
        scalars,
        (shared, features),
        adapt_in,
        adapt_out,
        [
            shaped((token_count, width), BF16),
            shaped((token_count, 640), BF16),
            shaped((token_count, width + 640), F32),
            shaped(adapt_in.shape[1:], BF16),
            shaped(adapt_out.shape[1:], BF16),
        ],
    )
    mixed, handed = lax.optimization_barrier((mixed, handed))
    grad_pred, grad_zeta, kept, given = call(
        functools.partial(adapt_backward_kernel, loss_scale),
        scalars,
        (sorter, arrived, mixed, first, second),
        [
            shaped((token_count, width), BF16),
            shaped((token_count, 640), BF16),
            shaped((half, width), F32),
            shaped((half, width), BF16),
        ],
    )

    came = send(given, swap_core)
    adapt_keep, adapt_give = call(
        functools.partial(adapt_partial_kernel, 3),
        scalars,
        (student, grad_zeta, gamma, grad_pred),
        [shaped((2, 8, 40, 1280), BF16)] * 2,
        [pltpu.VMEM((32, 40, 1280), F32)],
        24,
        4 * token_count * width * 640,
    )
    came, adapt_keep = lax.optimization_barrier((came, adapt_keep))
    pair, pair_b = call(
        pair_kernel,
        scalars,
        (kept, came),
        [shaped((half, width), F32), shaped((half, width), BF16)],
    )
    pair, hidden_crossed = lax.optimization_barrier((pair, hidden_crossed))
    hidden_core = send(hidden_crossed, swap_core)
    across = send(pair_b, exchange_across)
    left, slopes, weights = stage(
        scalars, (hidden_crossed, hidden_core, hand, handed, slope, block_out)
    )
    across, left = lax.optimization_barrier((across, left))
    adapt_came = send(adapt_give, first_axis(3))
    (mine,) = call(half_kernel, scalars, (pair, across), [shaped((half, width), BF16)])
    other = send(mine, swap_core)
    keep_a, give_a, keep_b, give_b = student_partial(
        scalars, (left, slopes, weights), mine, other
    )
    piece, low, grad_first, grad_second = both_axes(
        scalars, keep_a, give_a, keep_b, give_b, adapt_keep, adapt_came
    )
    grad_second = jnp.swapaxes(grad_second, 0, 1)
    grad_in_sum, grad_out_sum = call(
        last_kernel,
        scalars,
        (piece, low),
        [shaped((1, 40, 2560), F32), shaped((1, 80, 1280), F32)],
    )
    return (grad_first, grad_second, grad_in_sum, grad_out_sum)


def solution(mesh):
    fine = Mesh(mesh.devices.reshape(SIZES), ALL)
    placed = (
        P(GROUP, WIDE, None),
        P(GROUP, None, None),
        P(GROUP, None, None),
        P(),
        P(),
        P(),
    )
    return jax.shard_map(
        body,
        mesh=fine,
        in_specs=placed,
        out_specs=(P(GROUP, WIDE, None),) * 4,
        check_vma=False,
    )
```
